32 devices in a mesh: samples: 4 (over y, x), space: 8 (over z, core).
Axes of the slice: x: 2, y: 2, z: 4, core: 2. Of those that a mesh axis runs over, the one named last changes fastest.
Arguments:
- target: bfloat16 [8, 8192, 4096], P(None, 'samples', 'space'), may hold values from 0 to 1
- a_factor: bfloat16 [8192, 256], P(('samples', 'space')), may hold values from -3 to 3
- b_factor: bfloat16 [4096, 256], P(('space', 'samples')), may hold values from -3 to 3
- c_factor: bfloat16 [8, 256], replicated, may hold values from -3 to 3
Outputs:
- grad_a: float32 [8192, 256], P(('samples', 'space'))
- grad_b: float32 [4096, 256], P(('space', 'samples'))
- grad_c: float32 [8, 256], replicated
The draws below stay inside these ranges and needn't reach their ends.
All inputs are finite; a program needn't handle non-finite values.
Results may differ from the reference program's by a relative error of at most 0.002.
Values may be sent and summed in bfloat16 or wider, within the bound.
A program may use at most 128 MiB of HBM per device.

```python
import jax
import jax.numpy as jnp
from jax import lax

R = 256
K = 8
I = 8192
J = 4096


def block_scale(rng, dims, shards, low, top_value):
    level = 1.0
    for dim, shards_of in shards:
        steps = jax.random.uniform(jax.random.fold_in(jax.random.fold_in(rng, 6), dim), (shards_of,), jnp.float32, low / len(shards), top_value / len(shards))
        level = level * jnp.repeat(jnp.exp(steps), dims[dim] // shards_of).reshape((-1,) + (1,) * (len(dims) - 1 - dim))
    return level


def normal_values(rng, shape, scale, reach, pieces=(), kind=jnp.bfloat16):
    entries = scale * jax.random.normal(rng, shape, jnp.float32)
    if pieces:
        entries = entries * block_scale(rng, shape, pieces, -0.22, 0.18)
    return jnp.clip(entries, -reach, reach).astype(kind)


def setup_inputs(seed: int = 0) -> dict:
    streams_of = jax.random.split(jax.random.key(seed), 5)
    return {
        "target": jnp.clip(1.0 * jax.random.uniform(streams_of[0], (K, I, J), jnp.float32) ** block_scale(streams_of[0], (K, I, J), ((1, 4), (2, 8)), -0.2, 0.2), 0.0, 1.0).astype(jnp.bfloat16),
        "a_factor": normal_values(streams_of[1], (I, R), 0.5, 3.0, ((0, 32),)),
        "b_factor": normal_values(streams_of[2], (J, R), 0.5, 3.0, ((0, 32),)),
        "c_factor": normal_values(streams_of[3], (K, R), 0.5, 3.0),
    }


def reference(target, a_factor, b_factor, c_factor):
    b_wide = b_factor.astype(jnp.float32)
    a_wide = a_factor.astype(jnp.float32)

    def per_step(carry, inputs):
        grad_a, grad_b = carry
        slab, c_row = inputs
        c_wide = c_row.astype(jnp.float32)
        scaled = (a_wide * c_wide[None, :]).astype(jnp.bfloat16)
        model = jnp.dot(scaled, b_factor.T, preferred_element_type=jnp.float32)
        derivative = (jax.nn.sigmoid(model) - slab.astype(jnp.float32)).astype(jnp.bfloat16)
        inner = jnp.dot(derivative, b_factor, preferred_element_type=jnp.float32)
        weighted = jnp.dot(derivative.T, a_factor, preferred_element_type=jnp.float32)
        grad_a = grad_a + inner * c_wide[None, :]
        grad_b = grad_b + weighted * c_wide[None, :]
        grad_c_row = jnp.sum(weighted * b_wide, axis=0)
        return (grad_a, grad_b), grad_c_row

    start = (jnp.zeros(a_factor.shape, jnp.float32), jnp.zeros(b_factor.shape, jnp.float32))
    (grad_a, grad_b), grad_c = lax.scan(per_step, start, (target, c_factor))
    return grad_a, grad_b, grad_c
```

```python
import functools

import jax
import jax.numpy as jnp
from jax import lax
from jax.experimental import pallas as pl
from jax.experimental.pallas import tpu as pltpu
from jax.sharding import PartitionSpec as P

MESH = pl.DeviceIdType.MESH
F32 = jnp.float32
BF16 = jnp.bfloat16
GROUP = 4


def matmul(x, y):
    return jnp.dot(x, y, preferred_element_type=F32)


def kernel(
    n_samples, n_space,
    target, a_own, b_own, c_ref,
    grad_a, grad_b, grad_c,
    t_buf, a_buf, b_buf, b_turned, c_down, c_along,
    d_buf0, d_buf1, s_buf0, s_buf1,
    sum_b, sum_c, part, sib_part, z_out, z_in, b_out, b_in, c_in, c_all,
    t_sem, a_recv, b_recv, b_send, a_send, fwd_send,
    sib_send, sib_recv, z_send, z_recv, gb_send, gb_recv,
    gc_send, gc_recv, gd_send, gd_recv,
):
    steps, width = c_ref.shape
    own_a = a_own.shape[0]
    own_b = b_own.shape[0]
    chips = n_space // 2
    m = lax.axis_index("samples")
    s = lax.axis_index("space")
    z, core = lax.div(s, 2), lax.rem(s, 2)
    sibling = z * 2 + 1 - core

    def other(d):
        found, bit = 0, 1
        while bit < chips:
            found = found + bit * lax.rem(lax.div(z, bit) + lax.div(jnp.int32(d), bit), 2)
            bit *= 2
        return found

    def block_at(t):
        pair, half = lax.div(t, 2), lax.rem(t, 2)
        flip = lax.div(pair + 1, chips)
        return other(lax.rem(pair + 1, chips)) * 2 + lax.rem(core + half + flip, 2)

    def load(t):
        rows = pl.ds(pl.multiple_of(block_at(t) * own_a, own_a), own_a)
        return pltpu.make_async_copy(target.at[:, rows, :], t_buf.at[t], t_sem.at[t])

    def send(src, dst, send_sem, recv_sem, **where):
        return pltpu.make_async_remote_copy(
            src_ref=src, dst_ref=dst, send_sem=send_sem, recv_sem=recv_sem,
            device_id=where, device_id_type=MESH,
        )

    def arrived(buf, sem):
        pltpu.make_async_copy(buf, buf, sem).wait()

    def send_b(i):
        return send(b_own, b_buf.at[m], b_send.at[i], b_recv.at[m], samples=lax.rem(m + i, n_samples))

    def send_a(d):
        to = sibling if d == 0 else other(d) * 2 + core
        return send(a_own, a_buf.at[s], a_send.at[d], a_recv.at[s], space=to)

    def send_far(d):
        return send(a_own, a_buf.at[s], a_send.at[d], a_recv.at[s], space=other(d) * 2 + core)

    def forward(t):
        block = a_buf.at[block_at(t)]
        return send(block, block, fwd_send.at[lax.div(t, 2)], a_recv.at[block_at(t)], space=sibling)

    def to_sibling(t, pair):
        return send(part.at[t], sib_part.at[pair], sib_send.at[pair], sib_recv.at[pair], space=sibling)

    def to_owner(pair):
        return send(
            z_out.at[pair], z_in.at[pair], z_send.at[pair], z_recv.at[pair],
            space=other(pair + 1) * 2 + core,
        )

    def send_gb(i):
        to = lax.rem(m + i, n_samples)
        return send(b_out.at[to], b_in.at[m], gb_send.at[i], gb_recv.at[m], samples=to)

    def send_gc(i):
        return send(c_in.at[m], c_in.at[m], gc_send.at[i], gc_recv.at[m], samples=lax.rem(m + i, n_samples))

    def send_gd(i):
        return send(c_all.at[s], c_all.at[s], gd_send.at[i], gd_recv.at[s], space=lax.rem(s + i, n_space))

    barrier = pltpu.get_barrier_semaphore()
    for i in range(1, n_samples):
        pl.semaphore_signal(barrier, inc=1, device_id={"samples": lax.rem(m + i, n_samples)}, device_id_type=MESH)
    for i in range(1, n_space):
        pl.semaphore_signal(barrier, inc=1, device_id={"space": lax.rem(s + i, n_space)}, device_id_type=MESH)
    own_b_copy = pltpu.make_async_copy(b_own, b_buf.at[m], b_recv.at[m])
    own_b_copy.start()
    own_a_copy = pltpu.make_async_copy(a_own, a_buf.at[s], a_recv.at[s])
    own_a_copy.start()
    load(jnp.int32(0)).start()
    pl.semaphore_wait(barrier, n_samples + n_space - 2)

    for i in range(1, n_samples):
        send_b(i).start()
    send_a(1).start()
    send_a(0).start()

    def start_load(t, carry):
        load(t).start()
        return carry

    lax.fori_loop(1, n_space, start_load, 0)

    c_wide = c_ref[...].astype(F32)
    c_turned = c_wide.T
    for k in range(steps):
        c_along[k] = jnp.broadcast_to(c_wide[k:k + 1, :], (own_a, width)).astype(BF16)
        c_down[k] = jnp.broadcast_to(c_turned[:, k:k + 1], (width, own_a)).astype(BF16)
    sum_b[...] = jnp.zeros_like(sum_b)
    sum_c[...] = jnp.zeros_like(sum_c)

    def wait_b(i, carry):
        arrived(b_buf.at[i], b_recv.at[i])
        return carry

    lax.fori_loop(0, n_samples, wait_b, 0)
    if chips > 2:
        send_a(2).start()
    b_all = b_buf[...].reshape(n_samples * own_b, width)
    b_turned[...] = (b_all.astype(F32) * 0.5).T.astype(BF16)

    def step(t, carry):
        pair = lax.div(t, 2)
        even = lax.rem(t, 2) == 0
        block = block_at(t)
        arrived(a_buf.at[block], a_recv.at[block])

        @pl.when(jnp.logical_and(even, t < n_space - 2))
        def _():
            forward(t).start()

        @pl.when(jnp.logical_and(even, pair + 3 < chips))
        def _():
            send_far(pair + 3).start()

        load(t).wait()
        a = a_buf[block]
        a_wide = a.astype(F32)
        a_turned = a_wide.T.astype(BF16)
        b_full = b_buf[...].reshape(n_samples * own_b, width)
        total = jnp.zeros((own_a, width), F32)
        for g, (d_buf, s_buf) in enumerate(((d_buf0, s_buf0), (d_buf1, s_buf1))):
            for j in range(GROUP):
                k = g * GROUP + j
                rows = slice(j * own_a, (j + 1) * own_a)
                half_model = matmul(a * c_along[k], b_turned[...])
                derivative = (0.5 * jnp.tanh(half_model) + (0.5 - t_buf[t, k].astype(F32))).astype(BF16)
                d_buf[rows, :] = derivative
                s_buf[:, rows] = a_turned * c_down[k]
                inner = matmul(derivative, b_full)
                total = total + inner * c_ref[k:k + 1, :].astype(F32)
                sum_c[k] += jnp.sum((a_wide * inner).reshape(own_a // 8, 8, width), axis=0)
            sum_b[...] += matmul(s_buf[...], d_buf[...])
        part[t] = total

        last = t == n_space - 2

        @pl.when(jnp.logical_or(last, jnp.logical_and(jnp.logical_not(even), t < n_space - 2)))
        def _():
            to_sibling(t, pair).start()

        @pl.when(jnp.logical_and(even, t >= 2))
        def _():
            before = pair - 1
            arrived(sib_part.at[before], sib_recv.at[before])
            z_out[before] = (part[t - 2] + sib_part[before]).astype(BF16)
            to_owner(before).start()

        return carry

    lax.fori_loop(0, n_space, step, 0)

    for k in range(steps):
        c_in[m, pl.ds(k, 1), :] = jnp.sum(sum_c[k], axis=0, keepdims=True)
    for i in range(1, n_samples):
        send_gc(i).start()
    turned = sum_b[...].T
    b_out[...] = turned.astype(BF16).reshape(n_samples, own_b, width)
    for i in range(1, n_samples):
        send_gb(i).start()

    arrived(sib_part.at[chips - 1], sib_recv.at[chips - 1])
    total = part[n_space - 1] + sib_part[chips - 1]
    for pair in range(chips - 1):
        arrived(z_in.at[pair], z_recv.at[pair])
        total = total + z_in[pair].astype(F32)
    grad_a[...] = total

    for i in range(1, n_samples):
        came = lax.rem(m + i, n_samples)
        arrived(c_in.at[came], gc_recv.at[came])
    c_all[s] = jnp.sum(c_in[...], axis=0)
    for i in range(1, n_space):
        send_gd(i).start()

    total = b_out[m].astype(F32)
    for i in range(1, n_samples):
        came = lax.rem(m + i, n_samples)
        arrived(b_in.at[came], gb_recv.at[came])
        total = total + b_in[came].astype(F32)
    grad_b[...] = total

    for i in range(1, n_space):
        came = lax.rem(s + i, n_space)
        arrived(c_all.at[came], gd_recv.at[came])
    grad_c[...] = jnp.sum(c_all[...], axis=0)

    for i in range(1, n_samples):
        send_b(i).wait_send()
        send_gb(i).wait_send()
        send_gc(i).wait_send()
    for d in range(chips):
        send_a(d).wait_send()
    for pair in range(chips - 1):
        forward(jnp.int32(2 * pair)).wait_send()
        to_owner(pair).wait_send()
        to_sibling(2 * pair + 1, pair).wait_send()
    to_sibling(n_space - 2, chips - 1).wait_send()
    for i in range(1, n_space):
        send_gd(i).wait_send()


def on_device(n_samples, n_space, target, a_factor, b_factor, c_factor):
    steps, rows, columns = target.shape
    own_a, width = a_factor.shape
    own_b = b_factor.shape[0]
    chips = n_space // 2
    vmem, dma = pltpu.VMEM, pltpu.SemaphoreType.DMA
    flops = 6 * steps * rows * columns * width
    anywhere = pl.BlockSpec(memory_space=pl.ANY)
    inside = pl.BlockSpec(memory_space=pltpu.VMEM)
    return pl.pallas_call(
        functools.partial(kernel, n_samples, n_space),
        out_shape=(
            jax.ShapeDtypeStruct((own_a, width), F32),
            jax.ShapeDtypeStruct((own_b, width), F32),
            jax.ShapeDtypeStruct((steps, width), F32),
        ),
        in_specs=[anywhere, anywhere, anywhere, inside],
        out_specs=(inside, inside, inside),
        scratch_shapes=[
            vmem((n_space, steps, own_a, columns), BF16),
            vmem((n_space, own_a, width), BF16),
            vmem((n_samples, own_b, width), BF16),
            vmem((width, columns), BF16),
            vmem((steps, width, own_a), BF16),
            vmem((steps, own_a, width), BF16),
            vmem((GROUP * own_a, columns), BF16),
            vmem((GROUP * own_a, columns), BF16),
            vmem((width, GROUP * own_a), BF16),
            vmem((width, GROUP * own_a), BF16),
            vmem((width, columns), F32),
            vmem((steps, 8, width), F32),
            vmem((n_space, own_a, width), F32),
            vmem((chips, own_a, width), F32),
            vmem((chips, own_a, width), BF16),
            vmem((chips, own_a, width), BF16),
            vmem((n_samples, own_b, width), BF16),
            vmem((n_samples, own_b, width), BF16),
            vmem((n_samples, steps, width), F32),
            vmem((n_space, steps, width), F32),
            dma((n_space,)), dma((n_space,)), dma((n_samples,)), dma((n_samples,)),
            dma((chips,)), dma((chips,)),
            dma((chips,)), dma((chips,)), dma((chips,)), dma((chips,)),
            dma((n_samples,)), dma((n_samples,)),
            dma((n_samples,)), dma((n_samples,)),
            dma((n_space,)), dma((n_space,)),
        ],
        compiler_params=pltpu.CompilerParams(
            collective_id=0, has_side_effects=True, vmem_limit_bytes=56 * 1024 * 1024
        ),
        cost_estimate=pl.CostEstimate(
            flops=flops, bytes_accessed=target.size * 2, transcendentals=target.size
        ),
        name="cp_gradient",
    )(target, a_factor, b_factor, c_factor)


def solution(mesh):
    n_samples, n_space = mesh.shape["samples"], mesh.shape["space"]
    return jax.shard_map(
        functools.partial(on_device, n_samples, n_space),
        mesh=mesh,
        in_specs=(
            P(None, "samples", "space"),
            P(("samples", "space"), None),
            P(("space", "samples"), None),
            P(),
        ),
        out_specs=(P(("samples", "space"), None), P(("space", "samples"), None), P()),
        check_vma=False,
    )
```

```python
import functools

import jax
import jax.numpy as jnp
from jax import lax
from jax.experimental import pallas as pl
from jax.experimental.pallas import tpu as pltpu
from jax.sharding import PartitionSpec as P

MESH = pl.DeviceIdType.MESH
F32 = jnp.float32
BF16 = jnp.bfloat16
GROUP = 4
CHUNK = 32


def matmul(x, y):
    return jnp.dot(x, y, preferred_element_type=F32)


def kernel(
    n_samples, n_space,
    target, a_own, b_own, c_ref,
    grad_a, grad_b, grad_c,
    t_buf, a_buf, b_buf, b_half, b_turned, c_down, c_along,
    h_bufs, d_bufs, s_bufs, x_buf, inner_buf, a_turned, a_before,
    sum_b, sum_c, part, sib_part, z_out, z_in, b_out, b_in, c_in, c_all,
    t_sem, a_recv, b_recv, b_send, a_send, fwd_send,
    sib_send, sib_recv, z_send, z_recv, gb_send, gb_recv,
    gc_send, gc_recv, gd_send, gd_recv,
):
    steps, width = c_ref.shape
    own_a = a_own.shape[0]
    own_b = b_own.shape[0]
    chips = n_space // 2
    m = lax.axis_index("samples")
    s = lax.axis_index("space")
    z, core = lax.div(s, 2), lax.rem(s, 2)
    sibling = z * 2 + 1 - core

    def other(d):
        found, bit = 0, 1
        while bit < chips:
            found = found + bit * lax.rem(lax.div(z, bit) + lax.div(jnp.int32(d), bit), 2)
            bit *= 2
        return found

    def block_at(t):
        pair, half = lax.div(t, 2), lax.rem(t, 2)
        flip = lax.div(pair + 1, chips)
        return other(lax.rem(pair + 1, chips)) * 2 + lax.rem(core + half + flip, 2)

    def load(t):
        rows = pl.ds(pl.multiple_of(block_at(t) * own_a, own_a), own_a)
        return pltpu.make_async_copy(target.at[:, rows, :], t_buf.at[t], t_sem.at[t])

    def send(src, dst, send_sem, recv_sem, **where):
        return pltpu.make_async_remote_copy(
            src_ref=src, dst_ref=dst, send_sem=send_sem, recv_sem=recv_sem,
            device_id=where, device_id_type=MESH,
        )

    def arrived(buf, sem):
        pltpu.make_async_copy(buf, buf, sem).wait()

    def send_b(i):
        return send(b_own, b_buf.at[m], b_send.at[i], b_recv.at[m], samples=lax.rem(m + i, n_samples))

    def send_a(d):
        to = sibling if d == 0 else other(d) * 2 + core
        return send(a_own, a_buf.at[s], a_send.at[d], a_recv.at[s], space=to)

    def send_far(d):
        return send(a_own, a_buf.at[s], a_send.at[d], a_recv.at[s], space=other(d) * 2 + core)

    def forward(t):
        block = a_buf.at[block_at(t)]
        return send(block, block, fwd_send.at[lax.div(t, 2)], a_recv.at[block_at(t)], space=sibling)

    def to_sibling(t, pair):
        return send(part.at[t], sib_part.at[pair], sib_send.at[pair], sib_recv.at[pair], space=sibling)

    def to_owner(pair):
        return send(
            z_out.at[pair], z_in.at[pair], z_send.at[pair], z_recv.at[pair],
            space=other(pair + 1) * 2 + core,
        )

    def send_gb(i):
        to = lax.rem(m + i, n_samples)
        return send(b_out.at[to], b_in.at[m], gb_send.at[i], gb_recv.at[m], samples=to)

    def send_gc(i):
        return send(c_in.at[m], c_in.at[m], gc_send.at[i], gc_recv.at[m], samples=lax.rem(m + i, n_samples))

    def send_gd(i):
        return send(c_all.at[s], c_all.at[s], gd_send.at[i], gd_recv.at[s], space=lax.rem(s + i, n_space))

    barrier = pltpu.get_barrier_semaphore()
    for i in range(1, n_samples):
        pl.semaphore_signal(barrier, inc=1, device_id={"samples": lax.rem(m + i, n_samples)}, device_id_type=MESH)
    for i in range(1, n_space):
        pl.semaphore_signal(barrier, inc=1, device_id={"space": lax.rem(s + i, n_space)}, device_id_type=MESH)
    own_b_copy = pltpu.make_async_copy(b_own, b_buf.at[m], b_recv.at[m])
    own_b_copy.start()
    own_a_copy = pltpu.make_async_copy(a_own, a_buf.at[s], a_recv.at[s])
    own_a_copy.start()
    load(jnp.int32(0)).start()
    pl.semaphore_wait(barrier, n_samples + n_space - 2)

    for i in range(1, n_samples):
        send_b(i).start()
    send_a(1).start()
    send_a(0).start()

    def start_load(t, carry):
        load(t).start()
        return carry

    lax.fori_loop(1, n_space, start_load, 0)

    c_wide = c_ref[...].astype(F32)
    c_turned = c_wide.T
    for k in range(steps):
        c_along[k] = jnp.broadcast_to(c_wide[k:k + 1, :], (own_a, width)).astype(BF16)
        c_down[k] = jnp.broadcast_to(0.5 * c_turned[:, k:k + 1], (width, own_a)).astype(BF16)
    sum_b[...] = jnp.zeros_like(sum_b)
    sum_c[...] = jnp.zeros_like(sum_c)

    def wait_b(i, carry):
        arrived(b_buf.at[i], b_recv.at[i])
        return carry

    lax.fori_loop(0, n_samples, wait_b, 0)
    if chips > 2:
        send_a(2).start()
    b_all = b_buf[...].reshape(n_samples * own_b, width)
    b_wide = b_all.astype(F32) * 0.5
    b_half[...] = b_wide.astype(BF16)
    b_turned[...] = b_wide.T.astype(BF16)

    def take(t):
        arrived(a_buf.at[block_at(t)], a_recv.at[block_at(t)])

        @pl.when(jnp.logical_and(lax.rem(t, 2) == 0, t < n_space - 2))
        def _():
            forward(t).start()

        far = lax.div(t, 2) + 3

        @pl.when(jnp.logical_and(lax.rem(t, 2) == 0, far < chips))
        def _():
            send_far(far).start()

    def stage_model(t, g):
        a = a_buf[block_at(t)]
        for j in range(GROUP):
            x_buf[j * own_a:(j + 1) * own_a, :] = a * c_along[g * GROUP + j]
        h_bufs[g][...] = matmul(x_buf[...], b_turned[...])

    def stage_derivative(t, g):
        for j in range(GROUP):
            k = g * GROUP + j
            s_bufs[g][:, j * own_a:(j + 1) * own_a] = a_turned[...] * c_down[k]
            for r in range(0, own_a, CHUNK):
                rows = slice(j * own_a + r, j * own_a + r + CHUNK)
                entries = t_buf[t, k, r:r + CHUNK, :]
                shift = 1.0 - (entries + entries).astype(F32)
                d_bufs[g][rows, :] = (jnp.tanh(h_bufs[g][rows, :]) + shift).astype(BF16)

    def stage_sums(t, g, a_rows):
        inner_buf[...] = matmul(d_bufs[g][...], b_half[...])
        over_c = [jnp.zeros((8, width), F32) for _ in range(GROUP)]
        for r in range(0, own_a, CHUNK):
            a_wide = a_rows(r)
            total = part[t, r:r + CHUNK, :] if g else jnp.zeros((CHUNK, width), F32)
            for j in range(GROUP):
                k = g * GROUP + j
                inner = inner_buf[j * own_a + r:j * own_a + r + CHUNK, :]
                total = total + inner * c_ref[k:k + 1, :].astype(F32)
                product = a_wide * inner
                for q in range(0, CHUNK, 8):
                    over_c[j] = over_c[j] + product[q:q + 8, :]
            part[t, r:r + CHUNK, :] = total
        for j in range(GROUP):
            sum_c[g * GROUP + j] += over_c[j]
        sum_b[...] += matmul(s_bufs[g][...], d_bufs[g][...])

    def from_before(r):
        return a_before[r:r + CHUNK, :]

    def step(t, carry):
        before = lax.rem(t + n_space - 1, n_space)
        after = lax.rem(t + 1, n_space)
        block = block_at(t)
        load(t).wait()
        a_turned[...] = a_buf[block].astype(F32).T.astype(BF16)
        stage_model(t, 1)
        stage_derivative(t, 0)
        stage_sums(before, 1, from_before)

        @pl.when(t > 0)
        def _():
            pair = lax.div(before, 2)
            even = lax.rem(before, 2) == 0
            last = before == n_space - 2

            @pl.when(jnp.logical_or(last, jnp.logical_and(jnp.logical_not(even), before < n_space - 2)))
            def _():
                to_sibling(before, pair).start()

            @pl.when(jnp.logical_and(even, before >= 2))
            def _():
                ready = pair - 1
                arrived(sib_part.at[ready], sib_recv.at[ready])
                z_out[ready] = (part[before - 2] + sib_part[ready]).astype(BF16)
                to_owner(ready).start()

        @pl.when(t + 1 < n_space)
        def _():
            take(after)

        a_before[...] = a_buf[block].astype(F32)
        stage_model(after, 0)
        stage_derivative(t, 1)
        stage_sums(t, 0, lambda r: a_buf[block, r:r + CHUNK, :].astype(F32))
        return carry

    for buf in (d_bufs[1], s_bufs[1], a_before):
        buf[...] = jnp.zeros_like(buf)
    part[n_space - 1] = jnp.zeros((own_a, width), F32)
    take(jnp.int32(0))
    stage_model(jnp.int32(0), 0)
    lax.fori_loop(0, n_space, step, 0)
    stage_sums(n_space - 1, 1, from_before)

    for k in range(steps):
        c_in[m, pl.ds(k, 1), :] = jnp.sum(sum_c[k], axis=0, keepdims=True)
    for i in range(1, n_samples):
        send_gc(i).start()
    turned = sum_b[...].T
    b_out[...] = turned.astype(BF16).reshape(n_samples, own_b, width)
    for i in range(1, n_samples):
        send_gb(i).start()

    arrived(sib_part.at[chips - 1], sib_recv.at[chips - 1])
    total = part[n_space - 1] + sib_part[chips - 1]
    for pair in range(chips - 1):
        arrived(z_in.at[pair], z_recv.at[pair])
        total = total + z_in[pair].astype(F32)
    grad_a[...] = total

    for i in range(1, n_samples):
        came = lax.rem(m + i, n_samples)
        arrived(c_in.at[came], gc_recv.at[came])
    c_all[s] = jnp.sum(c_in[...], axis=0)
    for i in range(1, n_space):
        send_gd(i).start()

    total = b_out[m].astype(F32)
    for i in range(1, n_samples):
        came = lax.rem(m + i, n_samples)
        arrived(b_in.at[came], gb_recv.at[came])
        total = total + b_in[came].astype(F32)
    grad_b[...] = total

    for i in range(1, n_space):
        came = lax.rem(s + i, n_space)
        arrived(c_all.at[came], gd_recv.at[came])
    grad_c[...] = jnp.sum(c_all[...], axis=0)

    for i in range(1, n_samples):
        send_b(i).wait_send()
        send_gb(i).wait_send()
        send_gc(i).wait_send()
    for d in range(chips):
        send_a(d).wait_send()
    for pair in range(chips - 1):
        forward(jnp.int32(2 * pair)).wait_send()
        to_owner(pair).wait_send()
        to_sibling(2 * pair + 1, pair).wait_send()
    to_sibling(n_space - 2, chips - 1).wait_send()
    for i in range(1, n_space):
        send_gd(i).wait_send()


def hand_over(in_a, in_b, in_c, out_a, out_b, out_c, sem):
    pairs = ((in_a, out_a), (in_b, out_b), (in_c, out_c))
    copies = [pltpu.make_async_copy(x, y, sem.at[i]) for i, (x, y) in enumerate(pairs)]
    for copy in copies:
        copy.start()
    for copy in copies:
        copy.wait()


def on_device(n_samples, n_space, target, a_factor, b_factor, c_factor):
    steps, rows, columns = target.shape
    own_a, width = a_factor.shape
    own_b = b_factor.shape[0]
    chips = n_space // 2
    vmem, dma = pltpu.VMEM, pltpu.SemaphoreType.DMA
    flops = 6 * steps * rows * columns * width
    anywhere = pl.BlockSpec(memory_space=pl.ANY)
    inside = pl.BlockSpec(memory_space=pltpu.VMEM)
    grads = pl.pallas_call(
        functools.partial(kernel, n_samples, n_space),
        out_shape=(
            jax.ShapeDtypeStruct((own_a, width), F32),
            jax.ShapeDtypeStruct((own_b, width), F32),
            jax.ShapeDtypeStruct((steps, width), F32),
        ),
        in_specs=[anywhere, anywhere, anywhere, inside],
        out_specs=(inside, inside, inside),
        scratch_shapes=[
            vmem((n_space, steps, own_a, columns), BF16),
            vmem((n_space, own_a, width), BF16),
            vmem((n_samples, own_b, width), BF16),
            vmem((columns, width), BF16),
            vmem((width, columns), BF16),
            vmem((steps, width, own_a), BF16),
            vmem((steps, own_a, width), BF16),
            [vmem((GROUP * own_a, columns), F32)] * 2,
            [vmem((GROUP * own_a, columns), BF16)] * 2,
            [vmem((width, GROUP * own_a), BF16)] * 2,
            vmem((GROUP * own_a, width), BF16),
            vmem((GROUP * own_a, width), F32),
            vmem((width, own_a), BF16),
            vmem((own_a, width), F32),
            vmem((width, columns), F32),
            vmem((steps, 8, width), F32),
            vmem((n_space, own_a, width), F32),
            vmem((chips, own_a, width), F32),
            vmem((chips, own_a, width), BF16),
            vmem((chips, own_a, width), BF16),
            vmem((n_samples, own_b, width), BF16),
            vmem((n_samples, own_b, width), BF16),
            vmem((n_samples, steps, width), F32),
            vmem((n_space, steps, width), F32),
            dma((n_space,)), dma((n_space,)), dma((n_samples,)), dma((n_samples,)),
            dma((chips,)), dma((chips,)),
            dma((chips,)), dma((chips,)), dma((chips,)), dma((chips,)),
            dma((n_samples,)), dma((n_samples,)),
            dma((n_samples,)), dma((n_samples,)),
            dma((n_space,)), dma((n_space,)),
        ],
        compiler_params=pltpu.CompilerParams(
            collective_id=0, has_side_effects=True, vmem_limit_bytes=56 * 1024 * 1024
        ),
        cost_estimate=pl.CostEstimate(
            flops=flops, bytes_accessed=target.size * 2, transcendentals=target.size
        ),
        name="cp_gradient",
    )(target, a_factor, b_factor, c_factor)
    return pl.pallas_call(
        hand_over,
        out_shape=tuple(jax.ShapeDtypeStruct(g.shape, g.dtype) for g in grads),
        in_specs=[anywhere] * 3,
        out_specs=(anywhere,) * 3,
        scratch_shapes=[dma((3,))],
        compiler_params=pltpu.CompilerParams(vmem_limit_bytes=56 * 1024 * 1024),
        name="hand_over",
    )(*grads)


def solution(mesh):
    n_samples, n_space = mesh.shape["samples"], mesh.shape["space"]
    return jax.shard_map(
        functools.partial(on_device, n_samples, n_space),
        mesh=mesh,
        in_specs=(
            P(None, "samples", "space"),
            P(("samples", "space"), None),
            P(("space", "samples"), None),
            P(),
        ),
        out_specs=(P(("samples", "space"), None), P(("space", "samples"), None), P()),
        check_vma=False,
    )
```

```python
import functools

import jax
import jax.numpy as jnp
from jax import lax
from jax.experimental import pallas as pl
from jax.experimental.pallas import tpu as pltpu
from jax.sharding import PartitionSpec as P

MESH = pl.DeviceIdType.MESH
F32 = jnp.float32
BF16 = jnp.bfloat16
CHUNK = 32


def matmul(x, y):
    return jnp.dot(x, y, preferred_element_type=F32)


def kernel(
    n_samples, n_space,
    target, a_own, b_own, c_ref,
    grad_a, grad_b, grad_c,
    t_buf, a_buf, b_buf, b_half, b_turned, c_down, c_along,
    d_bufs, s_bufs,
    sum_b, sum_c, part, sib_part, z_out, z_in, b_out, b_in, c_in, c_all,
    t_sem, a_recv, b_recv, b_send, a_send, fwd_send,
    sib_send, sib_recv, z_send, z_recv, gb_send, gb_recv,
    gc_send, gc_recv, gd_send, gd_recv,
):
    steps, width = c_ref.shape
    own_a = a_own.shape[0]
    own_b = b_own.shape[0]
    chips = n_space // 2
    m = lax.axis_index("samples")
    s = lax.axis_index("space")
    z, core = lax.div(s, 2), lax.rem(s, 2)
    sibling = z * 2 + 1 - core

    def other(d):
        found, bit = 0, 1
        while bit < chips:
            found = found + bit * lax.rem(lax.div(z, bit) + lax.div(jnp.int32(d), bit), 2)
            bit *= 2
        return found

    def block_at(t):
        pair, half = lax.div(t, 2), lax.rem(t, 2)
        flip = lax.div(pair + 1, chips)
        return other(lax.rem(pair + 1, chips)) * 2 + lax.rem(core + half + flip, 2)

    def load(t):
        rows = pl.ds(pl.multiple_of(block_at(t) * own_a, own_a), own_a)
        return pltpu.make_async_copy(target.at[:, rows, :], t_buf.at[t], t_sem.at[t])

    def send(src, dst, send_sem, recv_sem, **where):
        return pltpu.make_async_remote_copy(
            src_ref=src, dst_ref=dst, send_sem=send_sem, recv_sem=recv_sem,
            device_id=where, device_id_type=MESH,
        )

    def arrived(buf, sem):
        pltpu.make_async_copy(buf, buf, sem).wait()

    def send_b(i):
        return send(b_own, b_buf.at[m], b_send.at[i], b_recv.at[m], samples=lax.rem(m + i, n_samples))

    def send_a(d):
        to = sibling if d == 0 else other(d) * 2 + core
        return send(a_own, a_buf.at[s], a_send.at[d], a_recv.at[s], space=to)

    def send_far(d):
        return send(a_own, a_buf.at[s], a_send.at[d], a_recv.at[s], space=other(d) * 2 + core)

    def forward(t):
        block = a_buf.at[block_at(t)]
        return send(block, block, fwd_send.at[lax.div(t, 2)], a_recv.at[block_at(t)], space=sibling)

    def to_sibling(t, pair):
        return send(part.at[t], sib_part.at[pair], sib_send.at[pair], sib_recv.at[pair], space=sibling)

    def to_owner(pair):
        return send(
            z_out.at[pair], z_in.at[pair], z_send.at[pair], z_recv.at[pair],
            space=other(pair + 1) * 2 + core,
        )

    def send_gb(i):
        to = lax.rem(m + i, n_samples)
        return send(b_out.at[to], b_in.at[m], gb_send.at[i], gb_recv.at[m], samples=to)

    def send_gc(i):
        return send(c_in.at[m], c_in.at[m], gc_send.at[i], gc_recv.at[m], samples=lax.rem(m + i, n_samples))

    def send_gd(i):
        return send(c_all.at[s], c_all.at[s], gd_send.at[i], gd_recv.at[s], space=lax.rem(s + i, n_space))

    barrier = pltpu.get_barrier_semaphore()
    for i in range(1, n_samples):
        pl.semaphore_signal(barrier, inc=1, device_id={"samples": lax.rem(m + i, n_samples)}, device_id_type=MESH)
    for i in range(1, n_space):
        pl.semaphore_signal(barrier, inc=1, device_id={"space": lax.rem(s + i, n_space)}, device_id_type=MESH)
    own_b_copy = pltpu.make_async_copy(b_own, b_buf.at[m], b_recv.at[m])
    own_b_copy.start()
    own_a_copy = pltpu.make_async_copy(a_own, a_buf.at[s], a_recv.at[s])
    own_a_copy.start()
    load(jnp.int32(0)).start()
    pl.semaphore_wait(barrier, n_samples + n_space - 2)

    for i in range(1, n_samples):
        send_b(i).start()
    send_a(1).start()
    send_a(0).start()

    def start_load(t, carry):
        load(t).start()
        return carry

    lax.fori_loop(1, n_space, start_load, 0)

    c_wide = c_ref[...].astype(F32)
    c_turned = c_wide.T
    for k in range(steps):
        c_along[k] = jnp.broadcast_to(c_wide[k:k + 1, :], (own_a, width)).astype(BF16)
        c_down[k] = jnp.broadcast_to(0.5 * c_turned[:, k:k + 1], (width, own_a)).astype(BF16)
    sum_b[...] = jnp.zeros_like(sum_b)
    sum_c[...] = jnp.zeros_like(sum_c)

    def wait_b(i, carry):
        arrived(b_buf.at[i], b_recv.at[i])
        return carry

    lax.fori_loop(0, n_samples, wait_b, 0)
    if chips > 2:
        send_a(2).start()
    b_all = b_buf[...].reshape(n_samples * own_b, width)
    b_wide = b_all.astype(F32) * 0.5
    b_half[...] = b_wide.astype(BF16)
    b_turned[...] = b_wide.T.astype(BF16)

    def take(t):
        arrived(a_buf.at[block_at(t)], a_recv.at[block_at(t)])

        @pl.when(jnp.logical_and(lax.rem(t, 2) == 0, t < n_space - 2))
        def _():
            forward(t).start()

        far = lax.div(t, 2) + 3

        @pl.when(jnp.logical_and(lax.rem(t, 2) == 0, far < chips))
        def _():
            send_far(far).start()

    def step(t, carry):
        pair = lax.div(t, 2)
        even = lax.rem(t, 2) == 0
        block = block_at(t)
        take(t)
        load(t).wait()
        a = a_buf[block]
        a_wide = a.astype(F32)
        a_turned = a_wide.T.astype(BF16)

        def model(k):
            return matmul(a * c_along[k], b_turned[...])

        def slot(k):
            return k // 2 % 2, slice(k % 2 * own_a, (k % 2 + 1) * own_a)

        def derive(k, half_model):
            g, rows = slot(k)
            for r in range(0, own_a, CHUNK):
                entries = t_buf[t, k, r:r + CHUNK, :]
                shift = 1.0 - (entries + entries).astype(F32)
                found = (jnp.tanh(half_model[r:r + CHUNK]) + shift).astype(BF16)
                d_bufs[g][rows.start + r:rows.start + r + CHUNK, :] = found
            s_bufs[g][:, rows] = a_turned * c_down[k]

        def add_up(k, total):
            g, rows = slot(k)
            inner = matmul(d_bufs[g][rows, :], b_half[...])
            sum_c[k] += jnp.sum((a_wide * inner).reshape(own_a // 8, 8, width), axis=0)
            if k % 2:
                sum_b[...] += matmul(s_bufs[g][...], d_bufs[g][...])
            return total + inner * c_ref[k:k + 1, :].astype(F32)

        total = jnp.zeros((own_a, width), F32)
        now = model(0)
        for k in range(steps):
            later = model(k + 1) if k + 1 < steps else None
            derive(k, now)
            if k:
                total = add_up(k - 1, total)
            now = later
        part[t] = add_up(steps - 1, total)

        last = t == n_space - 2

        @pl.when(jnp.logical_or(last, jnp.logical_and(jnp.logical_not(even), t < n_space - 2)))
        def _():
            to_sibling(t, pair).start()

        @pl.when(jnp.logical_and(even, t >= 2))
        def _():
            before = pair - 1
            arrived(sib_part.at[before], sib_recv.at[before])
            z_out[before] = (part[t - 2] + sib_part[before]).astype(BF16)
            to_owner(before).start()

        return carry

    lax.fori_loop(0, n_space, step, 0)

    for k in range(steps):
        c_in[m, pl.ds(k, 1), :] = jnp.sum(sum_c[k], axis=0, keepdims=True)
    for i in range(1, n_samples):
        send_gc(i).start()
    turned = sum_b[...].T
    b_out[...] = turned.astype(BF16).reshape(n_samples, own_b, width)
    for i in range(1, n_samples):
        send_gb(i).start()

    arrived(sib_part.at[chips - 1], sib_recv.at[chips - 1])
    total = part[n_space - 1] + sib_part[chips - 1]
    for pair in range(chips - 1):
        arrived(z_in.at[pair], z_recv.at[pair])
        total = total + z_in[pair].astype(F32)
    grad_a[...] = total

    for i in range(1, n_samples):
        came = lax.rem(m + i, n_samples)
        arrived(c_in.at[came], gc_recv.at[came])
    c_all[s] = jnp.sum(c_in[...], axis=0)
    for i in range(1, n_space):
        send_gd(i).start()

    total = b_out[m].astype(F32)
    for i in range(1, n_samples):
        came = lax.rem(m + i, n_samples)
        arrived(b_in.at[came], gb_recv.at[came])
        total = total + b_in[came].astype(F32)
    grad_b[...] = total

    for i in range(1, n_space):
        came = lax.rem(s + i, n_space)
        arrived(c_all.at[came], gd_recv.at[came])
    grad_c[...] = jnp.sum(c_all[...], axis=0)

    for i in range(1, n_samples):
        send_b(i).wait_send()
        send_gb(i).wait_send()
        send_gc(i).wait_send()
    for d in range(chips):
        send_a(d).wait_send()
    for pair in range(chips - 1):
        forward(jnp.int32(2 * pair)).wait_send()
        to_owner(pair).wait_send()
        to_sibling(2 * pair + 1, pair).wait_send()
    to_sibling(n_space - 2, chips - 1).wait_send()
    for i in range(1, n_space):
        send_gd(i).wait_send()


def hand_over(in_a, in_b, in_c, out_a, out_b, out_c, via_a, via_b, via_c, sem):
    def copies(sources, targets):
        started = [pltpu.make_async_copy(x, y, sem.at[i]) for i, (x, y) in enumerate(zip(sources, targets))]
        for copy in started:
            copy.start()
        for copy in started:
            copy.wait()

    copies((in_a, in_b, in_c), (via_a, via_b, via_c))
    copies((via_a, via_b, via_c), (out_a, out_b, out_c))


def on_device(n_samples, n_space, target, a_factor, b_factor, c_factor):
    steps, rows, columns = target.shape
    own_a, width = a_factor.shape
    own_b = b_factor.shape[0]
    chips = n_space // 2
    vmem, dma = pltpu.VMEM, pltpu.SemaphoreType.DMA
    flops = 6 * steps * rows * columns * width
    anywhere = pl.BlockSpec(memory_space=pl.ANY)
    inside = pl.BlockSpec(memory_space=pltpu.VMEM)
    grads = pl.pallas_call(
        functools.partial(kernel, n_samples, n_space),
        out_shape=(
            jax.ShapeDtypeStruct((own_a, width), F32),
            jax.ShapeDtypeStruct((own_b, width), F32),
            jax.ShapeDtypeStruct((steps, width), F32),
        ),
        in_specs=[anywhere, anywhere, anywhere, inside],
        out_specs=(inside, inside, inside),
        scratch_shapes=[
            vmem((n_space, steps, own_a, columns), BF16),
            vmem((n_space, own_a, width), BF16),
            vmem((n_samples, own_b, width), BF16),
            vmem((columns, width), BF16),
            vmem((width, columns), BF16),
            vmem((steps, width, own_a), BF16),
            vmem((steps, own_a, width), BF16),
            [vmem((2 * own_a, columns), BF16)] * 2,
            [vmem((width, 2 * own_a), BF16)] * 2,
            vmem((width, columns), F32),
            vmem((steps, 8, width), F32),
            vmem((n_space, own_a, width), F32),
            vmem((chips, own_a, width), F32),
            vmem((chips, own_a, width), BF16),
            vmem((chips, own_a, width), BF16),
            vmem((n_samples, own_b, width), BF16),
            vmem((n_samples, own_b, width), BF16),
            vmem((n_samples, steps, width), F32),
            vmem((n_space, steps, width), F32),
            dma((n_space,)), dma((n_space,)), dma((n_samples,)), dma((n_samples,)),
            dma((chips,)), dma((chips,)),
            dma((chips,)), dma((chips,)), dma((chips,)), dma((chips,)),
            dma((n_samples,)), dma((n_samples,)),
            dma((n_samples,)), dma((n_samples,)),
            dma((n_space,)), dma((n_space,)),
        ],
        compiler_params=pltpu.CompilerParams(
            collective_id=0, has_side_effects=True, vmem_limit_bytes=56 * 1024 * 1024
        ),
        cost_estimate=pl.CostEstimate(
            flops=flops, bytes_accessed=target.size * 2, transcendentals=target.size
        ),
        name="cp_gradient",
    )(target, a_factor, b_factor, c_factor)
    return pl.pallas_call(
        hand_over,
        out_shape=tuple(jax.ShapeDtypeStruct(g.shape, g.dtype) for g in grads),
        in_specs=[anywhere] * 3,
        out_specs=(anywhere,) * 3,
        scratch_shapes=[vmem(g.shape, g.dtype) for g in grads] + [dma((3,))],
        compiler_params=pltpu.CompilerParams(vmem_limit_bytes=56 * 1024 * 1024),
        name="hand_over",
    )(*grads)


def solution(mesh):
    n_samples, n_space = mesh.shape["samples"], mesh.shape["space"]
    return jax.shard_map(
        functools.partial(on_device, n_samples, n_space),
        mesh=mesh,
        in_specs=(
            P(None, "samples", "space"),
            P(("samples", "space"), None),
            P(("space", "samples"), None),
            P(),
        ),
        out_specs=(P(("samples", "space"), None), P(("space", "samples"), None), P()),
        check_vma=False,
    )
```

```python
import functools

import jax
import jax.numpy as jnp
from jax import lax
from jax.experimental import pallas as pl
from jax.experimental.pallas import tpu as pltpu
from jax.sharding import PartitionSpec as P

MESH = pl.DeviceIdType.MESH
F32 = jnp.float32
BF16 = jnp.bfloat16
CHUNK = 32


def matmul(x, y):
    return jnp.dot(x, y, preferred_element_type=F32)


def kernel(
    n_samples, n_space,
    target, a_own, b_own, c_ref,
    grad_a, grad_b, grad_c,
    t_buf, a_buf, b_buf, b_half, b_turned, c_down, c_along,
    d_bufs, s_bufs,
    sum_b, sum_c, part, sib_part, z_out, z_in, b_out, b_in, c_in, c_all,
    t_sem, a_recv, b_recv, b_send, a_send, fwd_send,
    sib_send, sib_recv, z_send, z_recv, gb_send, gb_recv,
    gc_send, gc_recv, gd_send, gd_recv,
):
    steps, width = c_ref.shape
    own_a = a_own.shape[0]
    own_b = b_own.shape[0]
    chips = n_space // 2
    m = lax.axis_index("samples")
    s = lax.axis_index("space")
    z, core = lax.div(s, 2), lax.rem(s, 2)
    sibling = z * 2 + 1 - core

    def other(d):
        found, bit = 0, 1
        while bit < chips:
            found = found + bit * lax.rem(lax.div(z, bit) + lax.div(jnp.int32(d), bit), 2)
            bit *= 2
        return found

    def block_at(t):
        d, half = lax.rem(lax.div(t + 1, 2), chips), lax.rem(t + 1, 2)
        flip = lax.div(chips - d, chips)
        return other(d) * 2 + lax.rem(core + half + flip, 2)

    def load(t):
        rows = pl.ds(pl.multiple_of(block_at(t) * own_a, own_a), own_a)
        return pltpu.make_async_copy(target.at[:, rows, :], t_buf.at[t], t_sem.at[t])

    def send(src, dst, send_sem, recv_sem, **where):
        return pltpu.make_async_remote_copy(
            src_ref=src, dst_ref=dst, send_sem=send_sem, recv_sem=recv_sem,
            device_id=where, device_id_type=MESH,
        )

    def arrived(buf, sem):
        pltpu.make_async_copy(buf, buf, sem).wait()

    def send_b(i):
        return send(b_own, b_buf.at[m], b_send.at[i], b_recv.at[m], samples=lax.rem(m + i, n_samples))

    def send_a(d):
        to = sibling if d == 0 else other(d) * 2 + core
        return send(a_own, a_buf.at[s], a_send.at[d], a_recv.at[s], space=to)

    def forward(t):
        block = a_buf.at[block_at(t)]
        return send(block, block, fwd_send.at[lax.div(t, 2)], a_recv.at[block_at(t)], space=sibling)

    def to_sibling(t, pair):
        return send(part.at[t], sib_part.at[pair], sib_send.at[pair], sib_recv.at[pair], space=sibling)

    def to_owner(pair):
        return send(
            z_out.at[pair], z_in.at[pair], z_send.at[pair], z_recv.at[pair],
            space=other(pair + 1) * 2 + core,
        )

    def send_gb(i):
        to = lax.rem(m + i, n_samples)
        return send(b_out.at[to], b_in.at[m], gb_send.at[i], gb_recv.at[m], samples=to)

    def send_gc(i):
        return send(c_in.at[m], c_in.at[m], gc_send.at[i], gc_recv.at[m], samples=lax.rem(m + i, n_samples))

    def send_gd(i):
        return send(c_all.at[s], c_all.at[s], gd_send.at[i], gd_recv.at[s], space=lax.rem(s + i, n_space))

    barrier = pltpu.get_barrier_semaphore()
    for i in range(1, n_samples):
        pl.semaphore_signal(barrier, inc=1, device_id={"samples": lax.rem(m + i, n_samples)}, device_id_type=MESH)
    for i in range(1, n_space):
        pl.semaphore_signal(barrier, inc=1, device_id={"space": lax.rem(s + i, n_space)}, device_id_type=MESH)
    own_b_copy = pltpu.make_async_copy(b_own, b_buf.at[m], b_recv.at[m])
    own_b_copy.start()
    own_a_copy = pltpu.make_async_copy(a_own, a_buf.at[s], a_recv.at[s])
    own_a_copy.start()
    load(jnp.int32(0)).start()
    pl.semaphore_wait(barrier, n_samples + n_space - 2)

    for i in range(1, n_samples):
        send_b(i).start()
    for d in range(1, chips):
        send_a(d).start()
    send_a(0).start()

    def start_load(t, carry):
        load(t).start()
        return carry

    lax.fori_loop(1, n_space, start_load, 0)

    c_wide = c_ref[...].astype(F32)
    c_turned = c_wide.T
    for k in range(steps):
        c_along[k] = jnp.broadcast_to(c_wide[k:k + 1, :], (own_a, width)).astype(BF16)
        c_down[k] = jnp.broadcast_to(0.5 * c_turned[:, k:k + 1], (width, own_a)).astype(BF16)
    sum_b[...] = jnp.zeros_like(sum_b)
    sum_c[...] = jnp.zeros_like(sum_c)

    def wait_b(i, carry):
        arrived(b_buf.at[i], b_recv.at[i])
        return carry

    lax.fori_loop(0, n_samples, wait_b, 0)
    b_all = b_buf[...].reshape(n_samples * own_b, width)
    b_wide = b_all.astype(F32) * 0.5
    b_half[...] = b_wide.astype(BF16)
    b_turned[...] = b_wide.T.astype(BF16)

    def take(t):
        arrived(a_buf.at[block_at(t)], a_recv.at[block_at(t)])

        @pl.when(jnp.logical_and(lax.rem(t, 2) == 1, t < n_space - 1))
        def _():
            forward(t).start()

    def combine(t, odd):
        @pl.when(jnp.logical_and(odd, t >= 3))
        def _():
            ready = lax.div(t, 2) - 1
            arrived(sib_part.at[ready], sib_recv.at[ready])
            z_out[ready] = (part[t - 2] + sib_part[ready]).astype(BF16)
            to_owner(ready).start()

    def step(t, carry):
        odd = lax.rem(t, 2) == 1
        block = block_at(t)
        take(t)
        load(t).wait()
        a = a_buf[block]
        a_wide = a.astype(F32)
        a_turned = a_wide.T.astype(BF16)

        def model(k):
            return matmul(a * c_along[k], b_turned[...])

        def slot(k):
            return k // 2 % 2, slice(k % 2 * own_a, (k % 2 + 1) * own_a)

        def derive(k, half_model):
            g, rows = slot(k)
            for r in range(0, own_a, CHUNK):
                entries = t_buf[t, k, r:r + CHUNK, :]
                shift = 1.0 - (entries + entries).astype(F32)
                found = (jnp.tanh(half_model[r:r + CHUNK]) + shift).astype(BF16)
                d_bufs[g][rows.start + r:rows.start + r + CHUNK, :] = found
            s_bufs[g][:, rows] = a_turned * c_down[k]

        def add_up(k, total):
            g, rows = slot(k)
            inner = matmul(d_bufs[g][rows, :], b_half[...])
            sum_c[k] += jnp.sum((a_wide * inner).reshape(own_a // 8, 8, width), axis=0)
            if k % 2:
                sum_b[...] += matmul(s_bufs[g][...], d_bufs[g][...])
            return total + inner * c_ref[k:k + 1, :].astype(F32)

        total = jnp.zeros((own_a, width), F32)
        now = model(0)
        for k in range(steps):
            later = model(k + 1) if k + 1 < steps else None
            derive(k, now)
            if k:
                total = add_up(k - 1, total)
            now = later
            if k == steps // 2:
                combine(t, odd)
        part[t] = add_up(steps - 1, total)

        @pl.when(jnp.logical_or(t == n_space - 1, jnp.logical_and(jnp.logical_not(odd), t > 0)))
        def _():
            to_sibling(t, lax.div(t + 1, 2) - 1).start()

        return carry

    lax.fori_loop(0, n_space, step, 0)

    for k in range(steps):
        c_in[m, pl.ds(k, 1), :] = jnp.sum(sum_c[k], axis=0, keepdims=True)
    for i in range(1, n_samples):
        send_gc(i).start()
    turned = sum_b[...].T
    b_out[...] = turned.astype(BF16).reshape(n_samples, own_b, width)
    for i in range(1, n_samples):
        send_gb(i).start()

    arrived(sib_part.at[chips - 1], sib_recv.at[chips - 1])
    total = part[0] + sib_part[chips - 1]
    for pair in range(chips - 1):
        arrived(z_in.at[pair], z_recv.at[pair])
        total = total + z_in[pair].astype(F32)
    grad_a[...] = total

    for i in range(1, n_samples):
        came = lax.rem(m + i, n_samples)
        arrived(c_in.at[came], gc_recv.at[came])
    c_all[s] = jnp.sum(c_in[...], axis=0)
    for i in range(1, n_space):
        send_gd(i).start()

    total = b_out[m].astype(F32)
    for i in range(1, n_samples):
        came = lax.rem(m + i, n_samples)
        arrived(b_in.at[came], gb_recv.at[came])
        total = total + b_in[came].astype(F32)
    grad_b[...] = total

    for i in range(1, n_space):
        came = lax.rem(s + i, n_space)
        arrived(c_all.at[came], gd_recv.at[came])
    grad_c[...] = jnp.sum(c_all[...], axis=0)

    for i in range(1, n_samples):
        send_b(i).wait_send()
        send_gb(i).wait_send()
        send_gc(i).wait_send()
    for d in range(chips):
        send_a(d).wait_send()
    for pair in range(chips - 1):
        forward(jnp.int32(2 * pair + 1)).wait_send()
        to_owner(pair).wait_send()
        to_sibling(2 * pair + 2, pair).wait_send()
    to_sibling(n_space - 1, chips - 1).wait_send()
    for i in range(1, n_space):
        send_gd(i).wait_send()


def hand_over(in_a, in_b, in_c, out_a, out_b, out_c, via_a, via_b, via_c, sem):
    def copies(sources, targets):
        started = [pltpu.make_async_copy(x, y, sem.at[i]) for i, (x, y) in enumerate(zip(sources, targets))]
        for copy in started:
            copy.start()
        for copy in started:
            copy.wait()

    copies((in_a, in_b, in_c), (via_a, via_b, via_c))
    copies((via_a, via_b, via_c), (out_a, out_b, out_c))


def on_device(n_samples, n_space, target, a_factor, b_factor, c_factor):
    steps, rows, columns = target.shape
    own_a, width = a_factor.shape
    own_b = b_factor.shape[0]
    chips = n_space // 2
    vmem, dma = pltpu.VMEM, pltpu.SemaphoreType.DMA
    flops = 6 * steps * rows * columns * width
    anywhere = pl.BlockSpec(memory_space=pl.ANY)
    inside = pl.BlockSpec(memory_space=pltpu.VMEM)
    grads = pl.pallas_call(
        functools.partial(kernel, n_samples, n_space),
        out_shape=(
            jax.ShapeDtypeStruct((own_a, width), F32),
            jax.ShapeDtypeStruct((own_b, width), F32),
            jax.ShapeDtypeStruct((steps, width), F32),
        ),
        in_specs=[anywhere, anywhere, anywhere, inside],
        out_specs=(inside, inside, inside),
        scratch_shapes=[
            vmem((n_space, steps, own_a, columns), BF16),
            vmem((n_space, own_a, width), BF16),
            vmem((n_samples, own_b, width), BF16),
            vmem((columns, width), BF16),
            vmem((width, columns), BF16),
            vmem((steps, width, own_a), BF16),
            vmem((steps, own_a, width), BF16),
            [vmem((2 * own_a, columns), BF16)] * 2,
            [vmem((width, 2 * own_a), BF16)] * 2,
            vmem((width, columns), F32),
            vmem((steps, 8, width), F32),
            vmem((n_space, own_a, width), F32),
            vmem((chips, own_a, width), F32),
            vmem((chips, own_a, width), BF16),
            vmem((chips, own_a, width), BF16),
            vmem((n_samples, own_b, width), BF16),
            vmem((n_samples, own_b, width), BF16),
            vmem((n_samples, steps, width), F32),
            vmem((n_space, steps, width), F32),
            dma((n_space,)), dma((n_space,)), dma((n_samples,)), dma((n_samples,)),
            dma((chips,)), dma((chips,)),
            dma((chips,)), dma((chips,)), dma((chips,)), dma((chips,)),
            dma((n_samples,)), dma((n_samples,)),
            dma((n_samples,)), dma((n_samples,)),
            dma((n_space,)), dma((n_space,)),
        ],
        compiler_params=pltpu.CompilerParams(
            collective_id=0, has_side_effects=True, vmem_limit_bytes=56 * 1024 * 1024
        ),
        cost_estimate=pl.CostEstimate(
            flops=flops, bytes_accessed=target.size * 2, transcendentals=target.size
        ),
        name="cp_gradient",
    )(target, a_factor, b_factor, c_factor)
    return pl.pallas_call(
        hand_over,
        out_shape=tuple(jax.ShapeDtypeStruct(g.shape, g.dtype) for g in grads),
        in_specs=[anywhere] * 3,
        out_specs=(anywhere,) * 3,
        scratch_shapes=[vmem(g.shape, g.dtype) for g in grads] + [dma((3,))],
        compiler_params=pltpu.CompilerParams(vmem_limit_bytes=56 * 1024 * 1024),
        name="hand_over",
    )(*grads)


def solution(mesh):
    n_samples, n_space = mesh.shape["samples"], mesh.shape["space"]
    return jax.shard_map(
        functools.partial(on_device, n_samples, n_space),
        mesh=mesh,
        in_specs=(
            P(None, "samples", "space"),
            P(("samples", "space"), None),
            P(("space", "samples"), None),
            P(),
        ),
        out_specs=(P(("samples", "space"), None), P(("space", "samples"), None), P()),
        check_vma=False,
    )
```

```python
import functools

import jax
import jax.numpy as jnp
from jax import lax
from jax.experimental import pallas as pl
from jax.experimental.pallas import tpu as pltpu
from jax.sharding import PartitionSpec as P

MESH = pl.DeviceIdType.MESH
F32 = jnp.float32
BF16 = jnp.bfloat16
GROUP = 4
CHUNK = 32


def matmul(x, y):
    return jnp.dot(x, y, preferred_element_type=F32)


def kernel(
    n_samples, n_space,
    target, a_own, b_own, c_ref,
    grad_a, grad_b, grad_c,
    t_buf, a_buf, b_buf, b_half, b_turned, c_down, c_along,
    d_bufs, s_bufs,
    sum_b, sum_c, part, sib_part, z_out, z_in, b_out, b_in, c_in, c_all,
    t_sem, a_recv, b_recv, b_send, a_send, fwd_send,
    sib_send, sib_recv, z_send, z_recv, gb_send, gb_recv,
    gc_send, gc_recv, gd_send, gd_recv,
):
    steps, width = c_ref.shape
    own_a = a_own.shape[0]
    own_b = b_own.shape[0]
    chips = n_space // 2
    m = lax.axis_index("samples")
    s = lax.axis_index("space")
    z, core = lax.div(s, 2), lax.rem(s, 2)
    sibling = z * 2 + 1 - core

    def other(d):
        found, bit = 0, 1
        while bit < chips:
            found = found + bit * lax.rem(lax.div(z, bit) + lax.div(jnp.int32(d), bit), 2)
            bit *= 2
        return found

    def distance(turn):
        return lax.rem(turn, chips - 1) + lax.div(turn + chips - 1, chips) if chips > 1 else turn

    def block_at(t):
        turn, half = lax.rem(lax.div(t + 1, 2), chips), lax.rem(t + 1, 2)
        flip = lax.div(chips - turn, chips)
        return other(distance(turn)) * 2 + lax.rem(core + half + flip, 2)

    def load(t):
        rows = pl.ds(pl.multiple_of(block_at(t) * own_a, own_a), own_a)
        return pltpu.make_async_copy(target.at[:, rows, :], t_buf.at[t], t_sem.at[t])

    def send(src, dst, send_sem, recv_sem, **where):
        return pltpu.make_async_remote_copy(
            src_ref=src, dst_ref=dst, send_sem=send_sem, recv_sem=recv_sem,
            device_id=where, device_id_type=MESH,
        )

    def arrived(buf, sem):
        pltpu.make_async_copy(buf, buf, sem).wait()

    def send_b(i):
        return send(b_own, b_buf.at[m], b_send.at[i], b_recv.at[m], samples=lax.rem(m + i, n_samples))

    def send_a(d):
        to = sibling if d == 0 else other(d) * 2 + core
        return send(a_own, a_buf.at[s], a_send.at[d], a_recv.at[s], space=to)

    def forward(t):
        block = a_buf.at[block_at(t)]
        return send(block, block, fwd_send.at[lax.div(t, 2)], a_recv.at[block_at(t)], space=sibling)

    def to_sibling(t, pair):
        return send(part.at[t], sib_part.at[pair], sib_send.at[pair], sib_recv.at[pair], space=sibling)

    def to_owner(pair):
        return send(
            z_out.at[pair], z_in.at[pair], z_send.at[pair], z_recv.at[pair],
            space=other(distance(jnp.int32(pair + 1))) * 2 + core,
        )

    def send_gb(i):
        to = lax.rem(m + i, n_samples)
        return send(b_out.at[to], b_in.at[m], gb_send.at[i], gb_recv.at[m], samples=to)

    def send_gc(i):
        return send(c_in.at[m], c_in.at[m], gc_send.at[i], gc_recv.at[m], samples=lax.rem(m + i, n_samples))

    def send_gd(i):
        return send(c_all.at[s], c_all.at[s], gd_send.at[i], gd_recv.at[s], space=lax.rem(s + i, n_space))

    barrier = pltpu.get_barrier_semaphore()
    for i in range(1, n_samples):
        pl.semaphore_signal(barrier, inc=1, device_id={"samples": lax.rem(m + i, n_samples)}, device_id_type=MESH)
    for i in range(1, n_space):
        pl.semaphore_signal(barrier, inc=1, device_id={"space": lax.rem(s + i, n_space)}, device_id_type=MESH)
    own_b_copy = pltpu.make_async_copy(b_own, b_buf.at[m], b_recv.at[m])
    own_b_copy.start()
    own_a_copy = pltpu.make_async_copy(a_own, a_buf.at[s], a_recv.at[s])
    own_a_copy.start()
    load(jnp.int32(0)).start()
    pl.semaphore_wait(barrier, n_samples + n_space - 2)

    for i in range(1, n_samples):
        send_b(i).start()
    for turn in range(1, chips):
        send_a(turn % (chips - 1) + 1).start()
    send_a(0).start()

    def start_load(t, carry):
        load(t).start()
        return carry

    lax.fori_loop(1, n_space, start_load, 0)

    c_wide = c_ref[...].astype(F32)
    c_turned = c_wide.T
    for k in range(steps):
        c_along[k] = jnp.broadcast_to(c_wide[k:k + 1, :], (own_a, width)).astype(BF16)
        c_down[k] = jnp.broadcast_to(0.5 * c_turned[:, k:k + 1], (width, own_a)).astype(BF16)
    sum_b[...] = jnp.zeros_like(sum_b)
    sum_c[...] = jnp.zeros_like(sum_c)

    def wait_b(i, carry):
        arrived(b_buf.at[i], b_recv.at[i])
        return carry

    lax.fori_loop(0, n_samples, wait_b, 0)
    b_all = b_buf[...].reshape(n_samples * own_b, width)
    b_wide = b_all.astype(F32) * 0.5
    b_half[...] = b_wide.astype(BF16)
    b_turned[...] = b_wide.T.astype(BF16)

    def take(t):
        arrived(a_buf.at[block_at(t)], a_recv.at[block_at(t)])

        @pl.when(jnp.logical_and(lax.rem(t, 2) == 1, t < n_space - 1))
        def _():
            forward(t).start()

    def combine(t, odd):
        @pl.when(jnp.logical_and(odd, t >= 3))
        def _():
            ready = lax.div(t, 2) - 1
            arrived(sib_part.at[ready], sib_recv.at[ready])
            z_out[ready] = (part[t - 2] + sib_part[ready]).astype(BF16)
            to_owner(ready).start()

    def step(t, carry):
        odd = lax.rem(t, 2) == 1
        block = block_at(t)
        take(t)
        load(t).wait()
        a = a_buf[block]
        a_turned = a.astype(F32).T.astype(BF16)

        def derive(k):
            g, j = k // GROUP, k % GROUP
            half_model = matmul(a * c_along[k], b_turned[...])
            for r in range(0, own_a, CHUNK):
                entries = t_buf[t, k, r:r + CHUNK, :]
                shift = 1.0 - (entries + entries).astype(F32)
                found = (jnp.tanh(half_model[r:r + CHUNK]) + shift).astype(BF16)
                d_bufs[g][j * own_a + r:j * own_a + r + CHUNK, :] = found
            s_bufs[g][:, j * own_a:(j + 1) * own_a] = a_turned * c_down[k]

        def add_inner(k):
            g, j = k // GROUP, k % GROUP
            inner = matmul(d_bufs[g][j * own_a:(j + 2) * own_a, :], b_half[...])
            over_c = [jnp.zeros((8, width), F32)] * 2
            for r in range(0, own_a, CHUNK):
                a_rows = a_buf[block, r:r + CHUNK, :].astype(F32)
                total = part[t, r:r + CHUNK, :] if k else jnp.zeros((CHUNK, width), F32)
                for i in range(2):
                    piece = inner[i * own_a + r:i * own_a + r + CHUNK]
                    total = total + piece * c_ref[k + i:k + i + 1, :].astype(F32)
                    over_c[i] = over_c[i] + jnp.sum((a_rows * piece).reshape(CHUNK // 8, 8, width), axis=0)
                part[t, r:r + CHUNK, :] = total
            for i in range(2):
                sum_c[k + i] += over_c[i]

        def add_b(g):
            sum_b[...] += matmul(s_bufs[g][...], d_bufs[g][...])

        for k in range(0, steps, 2):
            if k == GROUP:
                combine(t, odd)
            derive(k)
            derive(k + 1)
            if k and k % GROUP == 0:
                add_b(k // GROUP - 1)
            add_inner(k)
        add_b(steps // GROUP - 1)

        @pl.when(jnp.logical_or(t == n_space - 1, jnp.logical_and(jnp.logical_not(odd), t > 0)))
        def _():
            to_sibling(t, lax.div(t + 1, 2) - 1).start()

        return carry

    lax.fori_loop(0, n_space, step, 0)

    for k in range(steps):
        c_in[m, pl.ds(k, 1), :] = jnp.sum(sum_c[k], axis=0, keepdims=True)
    for i in range(1, n_samples):
        send_gc(i).start()
    turned = sum_b[...].T
    b_out[...] = turned.astype(BF16).reshape(n_samples, own_b, width)
    for i in range(1, n_samples):
        send_gb(i).start()

    arrived(sib_part.at[chips - 1], sib_recv.at[chips - 1])
    total = part[0] + sib_part[chips - 1]
    for pair in range(chips - 1):
        arrived(z_in.at[pair], z_recv.at[pair])
        total = total + z_in[pair].astype(F32)
    grad_a[...] = total

    for i in range(1, n_samples):
        came = lax.rem(m + i, n_samples)
        arrived(c_in.at[came], gc_recv.at[came])
    c_all[s] = jnp.sum(c_in[...], axis=0)
    for i in range(1, n_space):
        send_gd(i).start()

    total = b_out[m].astype(F32)
    for i in range(1, n_samples):
        came = lax.rem(m + i, n_samples)
        arrived(b_in.at[came], gb_recv.at[came])
        total = total + b_in[came].astype(F32)
    grad_b[...] = total

    for i in range(1, n_space):
        came = lax.rem(s + i, n_space)
        arrived(c_all.at[came], gd_recv.at[came])
    grad_c[...] = jnp.sum(c_all[...], axis=0)

    for i in range(1, n_samples):
        send_b(i).wait_send()
        send_gb(i).wait_send()
        send_gc(i).wait_send()
    for d in range(chips):
        send_a(d).wait_send()
    for pair in range(chips - 1):
        forward(jnp.int32(2 * pair + 1)).wait_send()
        to_owner(pair).wait_send()
        to_sibling(2 * pair + 2, pair).wait_send()
    to_sibling(n_space - 1, chips - 1).wait_send()
    for i in range(1, n_space):
        send_gd(i).wait_send()


def hand_over(in_a, in_b, in_c, out_a, out_b, out_c, via_a, via_b, via_c, sem):
    def copies(sources, targets):
        started = [pltpu.make_async_copy(x, y, sem.at[i]) for i, (x, y) in enumerate(zip(sources, targets))]
        for copy in started:
            copy.start()
        for copy in started:
            copy.wait()

    copies((in_a, in_b, in_c), (via_a, via_b, via_c))
    copies((via_a, via_b, via_c), (out_a, out_b, out_c))


def on_device(n_samples, n_space, target, a_factor, b_factor, c_factor):
    steps, rows, columns = target.shape
    own_a, width = a_factor.shape
    own_b = b_factor.shape[0]
    chips = n_space // 2
    vmem, dma = pltpu.VMEM, pltpu.SemaphoreType.DMA
    flops = 6 * steps * rows * columns * width
    anywhere = pl.BlockSpec(memory_space=pl.ANY)
    inside = pl.BlockSpec(memory_space=pltpu.VMEM)
    grads = pl.pallas_call(
        functools.partial(kernel, n_samples, n_space),
        out_shape=(
            jax.ShapeDtypeStruct((own_a, width), F32),
            jax.ShapeDtypeStruct((own_b, width), F32),
            jax.ShapeDtypeStruct((steps, width), F32),
        ),
        in_specs=[anywhere, anywhere, anywhere, inside],
        out_specs=(inside, inside, inside),
        scratch_shapes=[
            vmem((n_space, steps, own_a, columns), BF16),
            vmem((n_space, own_a, width), BF16),
            vmem((n_samples, own_b, width), BF16),
            vmem((columns, width), BF16),
            vmem((width, columns), BF16),
            vmem((steps, width, own_a), BF16),
            vmem((steps, own_a, width), BF16),
            [vmem((GROUP * own_a, columns), BF16)] * (steps // GROUP),
            [vmem((width, GROUP * own_a), BF16)] * (steps // GROUP),
            vmem((width, columns), F32),
            vmem((steps, 8, width), F32),
            vmem((n_space, own_a, width), F32),
            vmem((chips, own_a, width), F32),
            vmem((chips, own_a, width), BF16),
            vmem((chips, own_a, width), BF16),
            vmem((n_samples, own_b, width), BF16),
            vmem((n_samples, own_b, width), BF16),
            vmem((n_samples, steps, width), F32),
            vmem((n_space, steps, width), F32),
            dma((n_space,)), dma((n_space,)), dma((n_samples,)), dma((n_samples,)),
            dma((chips,)), dma((chips,)),
            dma((chips,)), dma((chips,)), dma((chips,)), dma((chips,)),
            dma((n_samples,)), dma((n_samples,)),
            dma((n_samples,)), dma((n_samples,)),
            dma((n_space,)), dma((n_space,)),
        ],
        compiler_params=pltpu.CompilerParams(
            collective_id=0, has_side_effects=True, vmem_limit_bytes=56 * 1024 * 1024
        ),
        cost_estimate=pl.CostEstimate(
            flops=flops, bytes_accessed=target.size * 2, transcendentals=target.size
        ),
        name="cp_gradient",
    )(target, a_factor, b_factor, c_factor)
    return pl.pallas_call(
        hand_over,
        out_shape=tuple(jax.ShapeDtypeStruct(g.shape, g.dtype) for g in grads),
        in_specs=[anywhere] * 3,
        out_specs=(anywhere,) * 3,
        scratch_shapes=[vmem(g.shape, g.dtype) for g in grads] + [dma((3,))],
        compiler_params=pltpu.CompilerParams(vmem_limit_bytes=56 * 1024 * 1024),
        name="hand_over",
    )(*grads)


def solution(mesh):
    n_samples, n_space = mesh.shape["samples"], mesh.shape["space"]
    return jax.shard_map(
        functools.partial(on_device, n_samples, n_space),
        mesh=mesh,
        in_specs=(
            P(None, "samples", "space"),
            P(("samples", "space"), None),
            P(("space", "samples"), None),
            P(),
        ),
        out_specs=(P(("samples", "space"), None), P(("space", "samples"), None), P()),
        check_vma=False,
    )
```

```python
import functools

import jax
import jax.numpy as jnp
from jax import lax
from jax.experimental import pallas as pl
from jax.experimental.pallas import tpu as pltpu
from jax.sharding import PartitionSpec as P

MESH = pl.DeviceIdType.MESH
F32 = jnp.float32
BF16 = jnp.bfloat16
CHUNK = 32


def matmul(x, y):
    return jnp.dot(x, y, preferred_element_type=F32)


def kernel(
    n_samples, n_space,
    target, a_own, b_own, c_ref,
    grad_a, grad_b, grad_c,
    t_buf, a_buf, b_buf, b_half, b_turned, c_down, c_along,
    d_bufs, s_bufs,
    sum_b, sum_c, part, sib_part, z_out, z_in, b_out, b_in, c_in, c_all,
    t_sem, a_recv, b_recv, b_send, a_send, fwd_send,
    sib_send, sib_recv, z_send, z_recv, gb_send, gb_recv,
    gc_send, gc_recv, gd_send, gd_recv,
):
    steps, width = c_ref.shape
    own_a = a_own.shape[0]
    own_b = b_own.shape[0]
    chips = n_space // 2
    m = lax.axis_index("samples")
    s = lax.axis_index("space")
    z, core = lax.div(s, 2), lax.rem(s, 2)
    sibling = z * 2 + 1 - core

    def other(d):
        found, bit = 0, 1
        while bit < chips:
            found = found + bit * lax.rem(lax.div(z, bit) + lax.div(jnp.int32(d), bit), 2)
            bit *= 2
        return found

    def block_at(t):
        d, half = lax.rem(lax.div(t + 1, 2), chips), lax.rem(t + 1, 2)
        flip = lax.div(chips - d, chips)
        return other(d) * 2 + lax.rem(core + half + flip, 2)

    def load(t):
        rows = pl.ds(pl.multiple_of(block_at(t) * own_a, own_a), own_a)
        return pltpu.make_async_copy(target.at[:, rows, :], t_buf.at[t], t_sem.at[t])

    def send(src, dst, send_sem, recv_sem, **where):
        return pltpu.make_async_remote_copy(
            src_ref=src, dst_ref=dst, send_sem=send_sem, recv_sem=recv_sem,
            device_id=where, device_id_type=MESH,
        )

    def arrived(buf, sem):
        pltpu.make_async_copy(buf, buf, sem).wait()

    def send_b(i):
        return send(b_own, b_buf.at[m], b_send.at[i], b_recv.at[m], samples=lax.rem(m + i, n_samples))

    def send_a(d):
        to = sibling if d == 0 else other(d) * 2 + core
        return send(a_own, a_buf.at[s], a_send.at[d], a_recv.at[s], space=to)

    def forward(t):
        block = a_buf.at[block_at(t)]
        return send(block, block, fwd_send.at[lax.div(t, 2)], a_recv.at[block_at(t)], space=sibling)

    def to_sibling(t, pair):
        return send(part.at[t], sib_part.at[pair], sib_send.at[pair], sib_recv.at[pair], space=sibling)

    def to_owner(pair):
        return send(
            z_out.at[pair], z_in.at[pair], z_send.at[pair], z_recv.at[pair],
            space=other(pair + 1) * 2 + core,
        )

    def send_gb(i):
        to = lax.rem(m + i, n_samples)
        return send(b_out.at[to], b_in.at[m], gb_send.at[i], gb_recv.at[m], samples=to)

    def send_gc(i):
        return send(c_in.at[m], c_in.at[m], gc_send.at[i], gc_recv.at[m], samples=lax.rem(m + i, n_samples))

    def send_gd(i):
        return send(c_all.at[s], c_all.at[s], gd_send.at[i], gd_recv.at[s], space=lax.rem(s + i, n_space))

    barrier = pltpu.get_barrier_semaphore()
    for i in range(1, n_samples):
        pl.semaphore_signal(barrier, inc=1, device_id={"samples": lax.rem(m + i, n_samples)}, device_id_type=MESH)
    for i in range(1, n_space):
        pl.semaphore_signal(barrier, inc=1, device_id={"space": lax.rem(s + i, n_space)}, device_id_type=MESH)
    own_b_copy = pltpu.make_async_copy(b_own, b_buf.at[m], b_recv.at[m])
    own_b_copy.start()
    own_a_copy = pltpu.make_async_copy(a_own, a_buf.at[s], a_recv.at[s])
    own_a_copy.start()
    load(jnp.int32(0)).start()
    pl.semaphore_wait(barrier, n_samples + n_space - 2)

    for i in range(1, n_samples):
        send_b(i).start()
    for d in range(1, chips):
        send_a(d).start()
    send_a(0).start()

    def start_load(t, carry):
        load(t).start()
        return carry

    lax.fori_loop(1, n_space, start_load, 0)

    c_wide = c_ref[...].astype(F32)
    c_turned = c_wide.T
    for k in range(steps):
        c_along[k] = jnp.broadcast_to(c_wide[k:k + 1, :], (own_a, width)).astype(BF16)
        c_down[k] = jnp.broadcast_to(0.5 * c_turned[:, k:k + 1], (width, own_a)).astype(BF16)
    sum_b[...] = jnp.zeros_like(sum_b)
    sum_c[...] = jnp.zeros_like(sum_c)

    def wait_b(i, carry):
        arrived(b_buf.at[i], b_recv.at[i])
        return carry

    lax.fori_loop(0, n_samples, wait_b, 0)
    b_all = b_buf[...].reshape(n_samples * own_b, width)
    b_wide = b_all.astype(F32) * 0.5
    b_half[...] = b_wide.astype(BF16)
    b_turned[...] = b_wide.T.astype(BF16)

    def take(t):
        arrived(a_buf.at[block_at(t)], a_recv.at[block_at(t)])

        @pl.when(jnp.logical_and(lax.rem(t, 2) == 1, t < n_space - 1))
        def _():
            forward(t).start()

    def combine(t, odd):
        @pl.when(jnp.logical_and(odd, t >= 3))
        def _():
            ready = lax.div(t, 2) - 1
            arrived(sib_part.at[ready], sib_recv.at[ready])
            z_out[ready] = (part[t - 2] + sib_part[ready]).astype(BF16)
            to_owner(ready).start()

    columns = b_turned.shape[1]
    halves = (slice(0, columns // 2), slice(columns // 2, columns))

    def step(t, carry, peeled=False):
        odd = lax.rem(t, 2) == 1
        block = block_at(t)
        take(t)
        load(t).wait()
        a = a_buf[block]
        a_wide = a.astype(F32)
        a_turned = a_wide.T.astype(BF16)

        def model(k, part_of):
            return matmul(a * c_along[k], b_turned[:, part_of])

        def slot(k):
            return k // 2 % 2, slice(k % 2 * own_a, (k % 2 + 1) * own_a)

        def derive(k, half_model, part_of):
            g, rows = slot(k)
            for r in range(0, own_a, CHUNK):
                entries = t_buf[t, k, r:r + CHUNK, part_of]
                shift = 1.0 - (entries + entries).astype(F32)
                found = (jnp.tanh(half_model[r:r + CHUNK]) + shift).astype(BF16)
                d_bufs[g][rows.start + r:rows.start + r + CHUNK, part_of] = found

        def add_inner(k, total):
            g, rows = slot(k)
            inner = sum(matmul(d_bufs[g][rows, part_of], b_half[part_of, :]) for part_of in halves)
            sum_c[k] += jnp.sum((a_wide * inner).reshape(own_a // 8, 8, width), axis=0)
            return total + inner * c_ref[k:k + 1, :].astype(F32)

        def add_b(k, part_of):
            g, _ = slot(k)
            sum_b[:, part_of] += matmul(s_bufs[g][...], d_bufs[g][:, part_of])

        total = jnp.zeros((own_a, width), F32)
        now = [model(0, part_of) for part_of in halves]
        for k in range(steps + 1):
            later = []
            for part_of, found in zip(halves, now if now else (None, None)):
                if k + 1 < steps:
                    later.append(model(k + 1, part_of))
                if k < steps:
                    derive(k, found, part_of)
                if k and k % 2 == 0:
                    add_b(k - 1, part_of)
            if k < steps:
                g, rows = slot(k)
                s_bufs[g][:, rows] = a_turned * c_down[k]
            if k:
                total = add_inner(k - 1, total)
            now = later
            if peeled and k == steps // 2:
                combine(t, odd)
        part[t] = total

        @pl.when(jnp.logical_or(t == n_space - 1, jnp.logical_and(jnp.logical_not(odd), t > 0)))
        def _():
            to_sibling(t, lax.div(t + 1, 2) - 1).start()

        if not peeled:
            combine(t, odd)
        return carry

    lax.fori_loop(0, n_space - 1, step, 0)
    step(jnp.int32(n_space - 1), 0, peeled=True)

    for k in range(steps):
        c_in[m, pl.ds(k, 1), :] = jnp.sum(sum_c[k], axis=0, keepdims=True)
    for i in range(1, n_samples):
        send_gc(i).start()
    turned = sum_b[...].T
    b_out[...] = turned.astype(BF16).reshape(n_samples, own_b, width)
    for i in range(1, n_samples):
        send_gb(i).start()

    arrived(sib_part.at[chips - 1], sib_recv.at[chips - 1])
    total = part[0] + sib_part[chips - 1]
    for pair in range(chips - 1):
        arrived(z_in.at[pair], z_recv.at[pair])
        total = total + z_in[pair].astype(F32)
    grad_a[...] = total

    for i in range(1, n_samples):
        came = lax.rem(m + i, n_samples)
        arrived(c_in.at[came], gc_recv.at[came])
    c_all[s] = jnp.sum(c_in[...], axis=0)
    for i in range(1, n_space):
        send_gd(i).start()

    total = b_out[m].astype(F32)
    for i in range(1, n_samples):
        came = lax.rem(m + i, n_samples)
        arrived(b_in.at[came], gb_recv.at[came])
        total = total + b_in[came].astype(F32)
    grad_b[...] = total

    for i in range(1, n_space):
        came = lax.rem(s + i, n_space)
        arrived(c_all.at[came], gd_recv.at[came])
    grad_c[...] = jnp.sum(c_all[...], axis=0)

    for i in range(1, n_samples):
        send_b(i).wait_send()
        send_gb(i).wait_send()
        send_gc(i).wait_send()
    for d in range(chips):
        send_a(d).wait_send()
    for pair in range(chips - 1):
        forward(jnp.int32(2 * pair + 1)).wait_send()
        to_owner(pair).wait_send()
        to_sibling(2 * pair + 2, pair).wait_send()
    to_sibling(n_space - 1, chips - 1).wait_send()
    for i in range(1, n_space):
        send_gd(i).wait_send()


def hand_over(in_a, in_b, in_c, out_a, out_b, out_c, via_a, via_b, via_c, sem):
    def copies(sources, targets):
        started = [pltpu.make_async_copy(x, y, sem.at[i]) for i, (x, y) in enumerate(zip(sources, targets))]
        for copy in started:
            copy.start()
        for copy in started:
            copy.wait()

    copies((in_a, in_b, in_c), (via_a, via_b, via_c))
    copies((via_a, via_b, via_c), (out_a, out_b, out_c))


def on_device(n_samples, n_space, target, a_factor, b_factor, c_factor):
    steps, rows, columns = target.shape
    own_a, width = a_factor.shape
    own_b = b_factor.shape[0]
    chips = n_space // 2
    vmem, dma = pltpu.VMEM, pltpu.SemaphoreType.DMA
    flops = 6 * steps * rows * columns * width
    anywhere = pl.BlockSpec(memory_space=pl.ANY)
    inside = pl.BlockSpec(memory_space=pltpu.VMEM)
    grads = pl.pallas_call(
        functools.partial(kernel, n_samples, n_space),
        out_shape=(
            jax.ShapeDtypeStruct((own_a, width), F32),
            jax.ShapeDtypeStruct((own_b, width), F32),
            jax.ShapeDtypeStruct((steps, width), F32),
        ),
        in_specs=[anywhere, anywhere, anywhere, inside],
        out_specs=(inside, inside, inside),
        scratch_shapes=[
            vmem((n_space, steps, own_a, columns), BF16),
            vmem((n_space, own_a, width), BF16),
            vmem((n_samples, own_b, width), BF16),
            vmem((columns, width), BF16),
            vmem((width, columns), BF16),
            vmem((steps, width, own_a), BF16),
            vmem((steps, own_a, width), BF16),
            [vmem((2 * own_a, columns), BF16)] * 2,
            [vmem((width, 2 * own_a), BF16)] * 2,
            vmem((width, columns), F32),
            vmem((steps, 8, width), F32),
            vmem((n_space, own_a, width), F32),
            vmem((chips, own_a, width), F32),
            vmem((chips, own_a, width), BF16),
            vmem((chips, own_a, width), BF16),
            vmem((n_samples, own_b, width), BF16),
            vmem((n_samples, own_b, width), BF16),
            vmem((n_samples, steps, width), F32),
            vmem((n_space, steps, width), F32),
            dma((n_space,)), dma((n_space,)), dma((n_samples,)), dma((n_samples,)),
            dma((chips,)), dma((chips,)),
            dma((chips,)), dma((chips,)), dma((chips,)), dma((chips,)),
            dma((n_samples,)), dma((n_samples,)),
            dma((n_samples,)), dma((n_samples,)),
            dma((n_space,)), dma((n_space,)),
        ],
        compiler_params=pltpu.CompilerParams(
            collective_id=0, has_side_effects=True, vmem_limit_bytes=56 * 1024 * 1024
        ),
        cost_estimate=pl.CostEstimate(
            flops=flops, bytes_accessed=target.size * 2, transcendentals=target.size
        ),
        name="cp_gradient",
    )(target, a_factor, b_factor, c_factor)
    return pl.pallas_call(
        hand_over,
        out_shape=tuple(jax.ShapeDtypeStruct(g.shape, g.dtype) for g in grads),
        in_specs=[anywhere] * 3,
        out_specs=(anywhere,) * 3,
        scratch_shapes=[vmem(g.shape, g.dtype) for g in grads] + [dma((3,))],
        compiler_params=pltpu.CompilerParams(vmem_limit_bytes=56 * 1024 * 1024),
        name="hand_over",
    )(*grads)


def solution(mesh):
    n_samples, n_space = mesh.shape["samples"], mesh.shape["space"]
    return jax.shard_map(
        functools.partial(on_device, n_samples, n_space),
        mesh=mesh,
        in_specs=(
            P(None, "samples", "space"),
            P(("samples", "space"), None),
            P(("space", "samples"), None),
            P(),
        ),
        out_specs=(P(("samples", "space"), None), P(("space", "samples"), None), P()),
        check_vma=False,
    )
```

```python
import functools

import jax
import jax.numpy as jnp
from jax import lax
from jax.experimental import pallas as pl
from jax.experimental.pallas import tpu as pltpu
from jax.sharding import PartitionSpec as P

MESH = pl.DeviceIdType.MESH
F32 = jnp.float32
BF16 = jnp.bfloat16
CHUNK = 32


def matmul(x, y):
    return jnp.dot(x, y, preferred_element_type=F32)


def kernel(
    n_samples, n_space,
    target, a_own, b_own, c_ref,
    grad_a, grad_b, grad_c,
    t_buf, a_buf, b_buf, b_half, b_turned, c_down, c_along,
    d_bufs, s_bufs,
    sum_b, sum_c, part, sib_part, z_out, z_in, b_out, b_in, c_in, c_all,
    t_sem, a_recv, b_recv, b_send, a_send, fwd_send,
    sib_send, sib_recv, z_send, z_recv, gb_send, gb_recv,
    gc_send, gc_recv, gd_send, gd_recv,
):
    steps, width = c_ref.shape
    own_a = a_own.shape[0]
    own_b = b_own.shape[0]
    chips = n_space // 2
    m = lax.axis_index("samples")
    s = lax.axis_index("space")
    z, core = lax.div(s, 2), lax.rem(s, 2)
    sibling = z * 2 + 1 - core

    def other(d):
        found, bit = 0, 1
        while bit < chips:
            found = found + bit * lax.rem(lax.div(z, bit) + lax.div(jnp.int32(d), bit), 2)
            bit *= 2
        return found

    def block_at(t):
        d, half = lax.rem(lax.div(t + 1, 2), chips), lax.rem(t + 1, 2)
        flip = lax.div(chips - d, chips)
        return other(d) * 2 + lax.rem(core + half + flip, 2)

    def load(t):
        rows = pl.ds(pl.multiple_of(block_at(t) * own_a, own_a), own_a)
        return pltpu.make_async_copy(target.at[:, rows, :], t_buf.at[t], t_sem.at[t])

    def send(src, dst, send_sem, recv_sem, **where):
        return pltpu.make_async_remote_copy(
            src_ref=src, dst_ref=dst, send_sem=send_sem, recv_sem=recv_sem,
            device_id=where, device_id_type=MESH,
        )

    def arrived(buf, sem):
        pltpu.make_async_copy(buf, buf, sem).wait()

    def send_b(i):
        return send(b_own, b_buf.at[m], b_send.at[i], b_recv.at[m], samples=lax.rem(m + i, n_samples))

    def send_a(d):
        to = sibling if d == 0 else other(d) * 2 + core
        return send(a_own, a_buf.at[s], a_send.at[d], a_recv.at[s], space=to)

    def send_far(d):
        return send(a_own, a_buf.at[s], a_send.at[d], a_recv.at[s], space=other(d) * 2 + core)

    def forward(t):
        block = a_buf.at[block_at(t)]
        return send(block, block, fwd_send.at[lax.div(t, 2)], a_recv.at[block_at(t)], space=sibling)

    def to_sibling(t, pair):
        return send(part.at[t], sib_part.at[pair], sib_send.at[pair], sib_recv.at[pair], space=sibling)

    def to_owner(pair):
        return send(
            z_out.at[pair], z_in.at[pair], z_send.at[pair], z_recv.at[pair],
            space=other(pair + 1) * 2 + core,
        )

    def send_gb(i):
        to = lax.rem(m + i, n_samples)
        return send(b_out.at[to], b_in.at[m], gb_send.at[i], gb_recv.at[m], samples=to)

    def send_gc(i):
        return send(c_in.at[m], c_in.at[m], gc_send.at[i], gc_recv.at[m], samples=lax.rem(m + i, n_samples))

    def send_gd(i):
        return send(c_all.at[s], c_all.at[s], gd_send.at[i], gd_recv.at[s], space=lax.rem(s + i, n_space))

    barrier = pltpu.get_barrier_semaphore()
    for i in range(1, n_samples):
        pl.semaphore_signal(barrier, inc=1, device_id={"samples": lax.rem(m + i, n_samples)}, device_id_type=MESH)
    for i in range(1, n_space):
        pl.semaphore_signal(barrier, inc=1, device_id={"space": lax.rem(s + i, n_space)}, device_id_type=MESH)
    own_b_copy = pltpu.make_async_copy(b_own, b_buf.at[m], b_recv.at[m])
    own_b_copy.start()
    own_a_copy = pltpu.make_async_copy(a_own, a_buf.at[s], a_recv.at[s])
    own_a_copy.start()
    load(jnp.int32(0)).start()
    pl.semaphore_wait(barrier, n_samples + n_space - 2)

    for i in range(1, n_samples):
        send_b(i).start()
    send_a(1).start()
    send_a(0).start()

    def start_load(t, carry):
        load(t).start()
        return carry

    lax.fori_loop(1, n_space, start_load, 0)

    c_wide = c_ref[...].astype(F32)
    c_turned = c_wide.T
    for k in range(steps):
        c_along[k] = jnp.broadcast_to(c_wide[k:k + 1, :], (own_a, width)).astype(BF16)
        c_down[k] = jnp.broadcast_to(0.5 * c_turned[:, k:k + 1], (width, own_a)).astype(BF16)
    sum_b[...] = jnp.zeros_like(sum_b)
    sum_c[...] = jnp.zeros_like(sum_c)

    def wait_b(i, carry):
        arrived(b_buf.at[i], b_recv.at[i])
        return carry

    lax.fori_loop(0, n_samples, wait_b, 0)
    if chips > 2:
        send_a(2).start()
    b_all = b_buf[...].reshape(n_samples * own_b, width)
    b_wide = b_all.astype(F32) * 0.5
    b_half[...] = b_wide.astype(BF16)
    b_turned[...] = b_wide.T.astype(BF16)

    def take(t):
        arrived(a_buf.at[block_at(t)], a_recv.at[block_at(t)])

        @pl.when(jnp.logical_and(lax.rem(t, 2) == 1, t < n_space - 1))
        def _():
            forward(t).start()

        far = lax.div(t, 2) + 3

        @pl.when(jnp.logical_and(lax.rem(t, 2) == 1, far < chips))
        def _():
            send_far(far).start()

    def combine(t, odd):
        @pl.when(jnp.logical_and(odd, t >= 3))
        def _():
            ready = lax.div(t, 2) - 1
            arrived(sib_part.at[ready], sib_recv.at[ready])
            z_out[ready] = (part[t - 2] + sib_part[ready]).astype(BF16)
            to_owner(ready).start()

    def step(t, carry):
        odd = lax.rem(t, 2) == 1
        block = block_at(t)
        take(t)
        load(t).wait()
        a = a_buf[block]
        a_wide = a.astype(F32)
        a_turned = a_wide.T.astype(BF16)

        def model(k):
            return matmul(a * c_along[k], b_turned[...])

        def slot(k):
            return k // 2 % 2, slice(k % 2 * own_a, (k % 2 + 1) * own_a)

        def derive(k, half_model):
            g, rows = slot(k)
            for r in range(0, own_a, CHUNK):
                entries = t_buf[t, k, r:r + CHUNK, :]
                shift = 1.0 - (entries + entries).astype(F32)
                found = (jnp.tanh(half_model[r:r + CHUNK]) + shift).astype(BF16)
                d_bufs[g][rows.start + r:rows.start + r + CHUNK, :] = found
            s_bufs[g][:, rows] = a_turned * c_down[k]

        def add_up(k, total):
            g, rows = slot(k)
            inner = matmul(d_bufs[g][rows, :], b_half[...])
            sum_c[k] += jnp.sum((a_wide * inner).reshape(own_a // 8, 8, width), axis=0)
            if k % 2:
                sum_b[...] += matmul(s_bufs[g][...], d_bufs[g][...])
            return total + inner * c_ref[k:k + 1, :].astype(F32)

        total = jnp.zeros((own_a, width), F32)
        now = model(0)
        for k in range(steps):
            later = model(k + 1) if k + 1 < steps else None
            derive(k, now)
            if k:
                total = add_up(k - 1, total)
            now = later
            if k == steps // 2:
                combine(t, odd)
        part[t] = add_up(steps - 1, total)

        @pl.when(jnp.logical_or(t == n_space - 1, jnp.logical_and(jnp.logical_not(odd), t > 0)))
        def _():
            to_sibling(t, lax.div(t + 1, 2) - 1).start()

        return carry

    lax.fori_loop(0, n_space, step, 0)

    for k in range(steps):
        c_in[m, pl.ds(k, 1), :] = jnp.sum(sum_c[k], axis=0, keepdims=True)
    for i in range(1, n_samples):
        send_gc(i).start()
    turned = sum_b[...].T
    b_out[...] = turned.astype(BF16).reshape(n_samples, own_b, width)
    for i in range(1, n_samples):
        send_gb(i).start()

    arrived(sib_part.at[chips - 1], sib_recv.at[chips - 1])
    total = part[0] + sib_part[chips - 1]
    for pair in range(chips - 1):
        arrived(z_in.at[pair], z_recv.at[pair])
        total = total + z_in[pair].astype(F32)
    grad_a[...] = total

    for i in range(1, n_samples):
        came = lax.rem(m + i, n_samples)
        arrived(c_in.at[came], gc_recv.at[came])
    c_all[s] = jnp.sum(c_in[...], axis=0)
    for i in range(1, n_space):
        send_gd(i).start()

    total = b_out[m].astype(F32)
    for i in range(1, n_samples):
        came = lax.rem(m + i, n_samples)
        arrived(b_in.at[came], gb_recv.at[came])
        total = total + b_in[came].astype(F32)
    grad_b[...] = total

    for i in range(1, n_space):
        came = lax.rem(s + i, n_space)
        arrived(c_all.at[came], gd_recv.at[came])
    grad_c[...] = jnp.sum(c_all[...], axis=0)

    for i in range(1, n_samples):
        send_b(i).wait_send()
        send_gb(i).wait_send()
        send_gc(i).wait_send()
    for d in range(chips):
        send_a(d).wait_send()
    for pair in range(chips - 1):
        forward(jnp.int32(2 * pair + 1)).wait_send()
        to_owner(pair).wait_send()
        to_sibling(2 * pair + 2, pair).wait_send()
    to_sibling(n_space - 1, chips - 1).wait_send()
    for i in range(1, n_space):
        send_gd(i).wait_send()


def hand_over(in_a, in_b, in_c, out_a, out_b, out_c, via_a, via_b, via_c, sem):
    def copies(sources, targets):
        started = [pltpu.make_async_copy(x, y, sem.at[i]) for i, (x, y) in enumerate(zip(sources, targets))]
        for copy in started:
            copy.start()
        for copy in started:
            copy.wait()

    copies((in_a, in_b, in_c), (via_a, via_b, via_c))
    copies((via_a, via_b, via_c), (out_a, out_b, out_c))


def on_device(n_samples, n_space, target, a_factor, b_factor, c_factor):
    steps, rows, columns = target.shape
    own_a, width = a_factor.shape
    own_b = b_factor.shape[0]
    chips = n_space // 2
    vmem, dma = pltpu.VMEM, pltpu.SemaphoreType.DMA
    flops = 6 * steps * rows * columns * width
    anywhere = pl.BlockSpec(memory_space=pl.ANY)
    inside = pl.BlockSpec(memory_space=pltpu.VMEM)
    grads = pl.pallas_call(
        functools.partial(kernel, n_samples, n_space),
        out_shape=(
            jax.ShapeDtypeStruct((own_a, width), F32),
            jax.ShapeDtypeStruct((own_b, width), F32),
            jax.ShapeDtypeStruct((steps, width), F32),
        ),
        in_specs=[anywhere, anywhere, anywhere, inside],
        out_specs=(inside, inside, inside),
        scratch_shapes=[
            vmem((n_space, steps, own_a, columns), BF16),
            vmem((n_space, own_a, width), BF16),
            vmem((n_samples, own_b, width), BF16),
            vmem((columns, width), BF16),
            vmem((width, columns), BF16),
            vmem((steps, width, own_a), BF16),
            vmem((steps, own_a, width), BF16),
            [vmem((2 * own_a, columns), BF16)] * 2,
            [vmem((width, 2 * own_a), BF16)] * 2,
            vmem((width, columns), F32),
            vmem((steps, 8, width), F32),
            vmem((n_space, own_a, width), F32),
            vmem((chips, own_a, width), F32),
            vmem((chips, own_a, width), BF16),
            vmem((chips, own_a, width), BF16),
            vmem((n_samples, own_b, width), BF16),
            vmem((n_samples, own_b, width), BF16),
            vmem((n_samples, steps, width), F32),
            vmem((n_space, steps, width), F32),
            dma((n_space,)), dma((n_space,)), dma((n_samples,)), dma((n_samples,)),
            dma((chips,)), dma((chips,)),
            dma((chips,)), dma((chips,)), dma((chips,)), dma((chips,)),
            dma((n_samples,)), dma((n_samples,)),
            dma((n_samples,)), dma((n_samples,)),
            dma((n_space,)), dma((n_space,)),
        ],
        compiler_params=pltpu.CompilerParams(
            collective_id=0, has_side_effects=True, vmem_limit_bytes=56 * 1024 * 1024
        ),
        cost_estimate=pl.CostEstimate(
            flops=flops, bytes_accessed=target.size * 2, transcendentals=target.size
        ),
        name="cp_gradient",
    )(target, a_factor, b_factor, c_factor)
    return pl.pallas_call(
        hand_over,
        out_shape=tuple(jax.ShapeDtypeStruct(g.shape, g.dtype) for g in grads),
        in_specs=[anywhere] * 3,
        out_specs=(anywhere,) * 3,
        scratch_shapes=[vmem(g.shape, g.dtype) for g in grads] + [dma((3,))],
        compiler_params=pltpu.CompilerParams(vmem_limit_bytes=56 * 1024 * 1024),
        name="hand_over",
    )(*grads)


def solution(mesh):
    n_samples, n_space = mesh.shape["samples"], mesh.shape["space"]
    return jax.shard_map(
        functools.partial(on_device, n_samples, n_space),
        mesh=mesh,
        in_specs=(
            P(None, "samples", "space"),
            P(("samples", "space"), None),
            P(("space", "samples"), None),
            P(),
        ),
        out_specs=(P(("samples", "space"), None), P(("space", "samples"), None), P()),
        check_vma=False,
    )
```
